512 devices in a mesh: seq: 16 (over y, x), head: 32 (over z, core).
Axes of the slice: x: 4, y: 4, z: 16, core: 2. Of those that a mesh axis runs over, the one named last changes fastest.
Arguments:
- q_raw: bfloat16 [6144, 4096], P('seq', 'head'), may hold values from -300 to 300
- k_raw: bfloat16 [6144, 4096], P('seq', 'head'), may hold values from -300 to 300
- values: bfloat16 [6144, 4096], P('seq', 'head'), may hold values from -6 to 6
- out: bfloat16 [6144, 4096], P('seq', 'head'), may hold values from -6 to 6
- d_out: bfloat16 [6144, 4096], P('seq', 'head'), may hold values from -6 to 6
- q_gain: bfloat16 [4096], P('head'), may hold values from 0.25 to 1.75
- k_gain: bfloat16 [4096], P('head'), may hold values from 0.25 to 1.75
- order: int32 [16], replicated, may hold values from 0 to 15, each once
Outputs:
- d_q: bfloat16 [6144, 4096], P('seq', 'head')
- d_k: bfloat16 [6144, 4096], P('seq', 'head')
- d_v: bfloat16 [6144, 4096], P('seq', 'head')
The draws below stay inside these ranges and needn't reach their ends.
All inputs are finite; a program needn't handle non-finite values.
Results may differ from the reference program's by a relative error of at most 0.025.
Values may be sent and summed in bfloat16 or wider, within the bound.
No kernel may reach another device: no remote copies, remote signals or barrier semaphores. Data moves between devices by JAX's collectives and lax.ppermute only.
A program may use at most 64 MiB of HBM per device.

```python
import math
import jax
import jax.numpy as jnp
from jax import lax

HEAD_DIM = 128
GROUP = 384
HEADS = 32
TOKENS = 6144
N_SEQ = 16


def apply_scales(key, base, top):
    key_cols, key_rows = jax.random.split(key)
    head_of = jnp.arange(HEADS * HEAD_DIM) // HEAD_DIM
    ramp = jnp.exp(math.log(top) * head_of.astype(jnp.float32) / max(HEADS - 1, 1))
    noise = jnp.exp(jax.random.uniform(key_cols, (HEADS * HEAD_DIM,), jnp.float32, math.log(0.7), math.log(1.4)))
    rows = jnp.exp(jax.random.uniform(key_rows, (TOKENS, 1), jnp.float32, 0.0, math.log(10.0)))
    return (base * ramp[None, :] * noise[None, :] * rows).astype(jnp.bfloat16)


def draw_q_raw(key, part):
    key = jax.random.fold_in(key, 11)
    first, second = jax.random.split(key)
    base = jnp.clip(jax.random.normal(first, (TOKENS, HEADS * HEAD_DIM), jnp.float32), -4.0, 4.0)
    return apply_scales(second, base, 3.0)


def draw_k_raw(key, part):
    key = jax.random.fold_in(key, 12)
    first, second = jax.random.split(key)
    base = jnp.clip(jax.random.normal(first, (TOKENS, HEADS * HEAD_DIM), jnp.float32), -4.0, 4.0)
    return apply_scales(second, base, 1.0 / 3.0)


def shard_levels(stream_key, extent, cuts, low, high):
    def one(dim, shards_of):
        draws = jax.random.uniform(jax.random.fold_in(jax.random.fold_in(stream_key, 6), dim), (shards_of,), jnp.float32, low / len(cuts), high / len(cuts))
        return jnp.repeat(jnp.exp(draws), extent[dim] // shards_of).reshape((-1,) + (1,) * (len(extent) - dim - 1))

    level = one(*cuts[0])
    for cut in cuts[1:]:
        level = level * one(*cut)
    return level


def scatter_about(key, extent, deviation, limit, cuts=(), kind=jnp.bfloat16):
    result = jax.random.normal(key, extent, jnp.float32) * deviation
    if len(cuts) > 0:
        result = shard_levels(key, extent, cuts, -0.22, 0.18) * result
    return jnp.clip(result, min=-limit, max=limit).astype(kind)


def setup_inputs(seed: int = 0) -> dict:
    arg_keys = jax.random.split(jax.random.key(seed), 9)
    return {
        "q_raw": draw_q_raw(jax.random.fold_in(arg_keys[8], 71), 0),
        "k_raw": draw_k_raw(jax.random.fold_in(arg_keys[8], 71), 0),
        "values": scatter_about(arg_keys[2], (TOKENS, HEADS * HEAD_DIM), 1.0, 6.0, ((0, 16), (1, 32))),
        "out": scatter_about(arg_keys[3], (TOKENS, HEADS * HEAD_DIM), 1.0, 6.0, ((0, 16), (1, 32))),
        "d_out": scatter_about(arg_keys[4], (TOKENS, HEADS * HEAD_DIM), 1.0, 6.0, ((0, 16), (1, 32))),
        "q_gain": jnp.clip(1.0 + 0.15 * jax.random.normal(arg_keys[5], (HEADS * HEAD_DIM,), jnp.float32), 0.25, 1.75).astype(jnp.bfloat16),
        "k_gain": jnp.clip(1.0 + 0.15 * jax.random.normal(arg_keys[6], (HEADS * HEAD_DIM,), jnp.float32), 0.25, 1.75).astype(jnp.bfloat16),
        "order": jax.random.permutation(arg_keys[7], N_SEQ).astype(jnp.int32),
    }


EPSILON = 1e-06

def reference(q_raw, k_raw, values, out, d_out, q_gain, k_gain, order):
    feature_count = HEADS * HEAD_DIM
    reciprocal_root = HEAD_DIM ** (-0.5)
    q_float = q_raw.astype(jnp.float32)
    k_float = k_raw.astype(jnp.float32)
    q_rate = lax.rsqrt(lax.optimization_barrier(jnp.mean(q_float * q_float, axis=1)) + EPSILON)
    k_rate = lax.rsqrt(lax.optimization_barrier(jnp.mean(k_float * k_float, axis=1)) + EPSILON)
    q_scale = q_gain.astype(jnp.float32)
    k_scale = k_gain.astype(jnp.float32)
    q_norm = (q_float * q_rate[:, None] * q_scale).astype(jnp.bfloat16)
    k_norm = (k_float * k_rate[:, None] * k_scale).astype(jnp.bfloat16)
    group_of = order[jnp.arange(TOKENS, dtype=jnp.int32) // GROUP]
    visible = group_of[:, None] >= group_of[None, :]

    def one_head(head_index):
        offset = head_index * HEAD_DIM

        def column(array):
            return lax.dynamic_slice_in_dim(array, offset, HEAD_DIM, 1)
        q_head = column(q_norm)
        k_head = column(k_norm)
        v_head = column(values)
        o_head = column(out)
        g_head = column(d_out)
        scores = jnp.dot(q_head, k_head.T, preferred_element_type=jnp.float32) * reciprocal_root
        row_total = lax.optimization_barrier(jnp.sum(jnp.where(visible, jnp.exp(scores), 0.0), axis=1))
        probs = jnp.where(visible, jnp.exp(scores - jnp.log(row_total)[:, None]), 0.0)
        probs_low = probs.astype(jnp.bfloat16)
        delta = lax.optimization_barrier(jnp.sum(g_head.astype(jnp.float32) * o_head.astype(jnp.float32), axis=1))
        dprobs = jnp.dot(g_head, v_head.T, preferred_element_type=jnp.float32)
        dscores = (probs * (dprobs - delta[:, None])).astype(jnp.bfloat16)
        query_grad = jnp.dot(dscores, k_head, preferred_element_type=jnp.float32) * reciprocal_root
        score_grad_tile = dscores.astype(jnp.float32).reshape(N_SEQ, GROUP, TOKENS)
        query_tile = q_head.astype(jnp.float32).reshape(N_SEQ, GROUP, HEAD_DIM)
        key_pieces = (jnp.einsum('faz,fap->fzp', score_grad_tile, query_tile) * reciprocal_root).astype(jnp.bfloat16)
        key_grad = lax.optimization_barrier(jnp.sum(lax.optimization_barrier(key_pieces).astype(jnp.float32), axis=0))
        probability_tile = probs_low.astype(jnp.float32).reshape(N_SEQ, GROUP, TOKENS)
        output_grad_tile = g_head.astype(jnp.float32).reshape(N_SEQ, GROUP, HEAD_DIM)
        value_pieces = jnp.einsum('faz,fap->fzp', probability_tile, output_grad_tile).astype(jnp.bfloat16)
        value_grad = lax.optimization_barrier(jnp.sum(lax.optimization_barrier(value_pieces).astype(jnp.float32), axis=0))
        return (query_grad, key_grad, value_grad)
    query_all, key_all, value_all = lax.map(one_head, jnp.arange(HEADS, dtype=jnp.int32))

    def merge_heads(stacked):
        return jnp.transpose(stacked, (1, 0, 2)).reshape(TOKENS, feature_count)
    q_grad = merge_heads(query_all) * q_scale
    k_grad = merge_heads(key_all) * k_scale
    d_q = q_rate[:, None] * q_grad - q_float * (q_rate ** 3 * lax.optimization_barrier(jnp.sum(q_grad * q_float, axis=1)) / feature_count)[:, None]
    d_k = k_rate[:, None] * k_grad - k_float * (k_rate ** 3 * lax.optimization_barrier(jnp.sum(k_grad * k_float, axis=1)) / feature_count)[:, None]
    return (d_q.astype(jnp.bfloat16), d_k.astype(jnp.bfloat16), merge_heads(value_all).astype(jnp.bfloat16))
```

```python
import math

import jax
import jax.numpy as jnp
from jax import lax
from jax.experimental import pallas as pl
from jax.experimental.pallas import tpu as pltpu
from jax.sharding import Mesh, PartitionSpec as P

EPSILON = 1e-06
SIDE = 4
ROWS = 384
WIDTH = 128
PIECES = ROWS // WIDTH
HEAD = ("z", "c")
SEQ = ("y", "x")
F32 = jnp.float32
BF16 = jnp.bfloat16
ROOT = WIDTH ** (-0.5)
LOG2E = math.log2(math.e)


def shift(value, axis, steps):
    count = lax.axis_size(axis)
    return lax.ppermute(value, axis, [(i, (i + steps) % count) for i in range(count)])


def struct(shape, dtype):
    return jax.ShapeDtypeStruct(shape, dtype)


def call(kernel, out_shape, scratch=(), smem=0, limit=32):
    def run(*args):
        specs = [
            pl.BlockSpec(memory_space=pltpu.SMEM if i < smem else pltpu.VMEM)
            for i in range(len(args))
        ]
        return pl.pallas_call(
            kernel,
            out_shape=out_shape,
            in_specs=specs,
            out_specs=jax.tree.map(lambda _: pl.BlockSpec(memory_space=pltpu.VMEM), out_shape),
            scratch_shapes=scratch,
            compiler_params=pltpu.CompilerParams(vmem_limit_bytes=limit * 2**20),
        )(*args)

    return run


def column(row):
    return jnp.broadcast_to(row, (WIDTH, WIDTH)).T


def row_sums(block):
    return jnp.sum(block.T, axis=0, keepdims=True)


def dot(a, b, dims=(((1,), (0,)), ((), ()))):
    return lax.dot_general(a, b, dims, preferred_element_type=F32)


NT = (((1,), (1,)), ((), ()))
TN = (((0,), (0,)), ((), ()))


def squares_kernel(q_ref, k_ref, v_ref, o_ref, g_ref, msg_ref, delta_ref, qg_ref, kv_ref):
    part = jnp.zeros((8, WIDTH), F32)
    delta = jnp.zeros((8, WIDTH), F32)
    line = lax.broadcasted_iota(jnp.int32, (8, WIDTH), 0)
    for i in range(PIECES):
        rows = pl.ds(i * WIDTH, WIDTH)
        q = q_ref[rows, :].astype(F32)
        k = k_ref[rows, :].astype(F32)
        g = g_ref[rows, :].astype(F32)
        o = o_ref[rows, :].astype(F32)
        part = jnp.where(line == i, row_sums(q * q), part)
        part = jnp.where(line == PIECES + i, row_sums(k * k), part)
        delta = jnp.where(line == i, row_sums(g * o), delta)
    msg_ref[...] = jnp.broadcast_to(part[None], msg_ref.shape)
    delta_ref[...] = delta
    qg_ref[:ROWS, :] = q_ref[...]
    qg_ref[ROWS:, :] = g_ref[...]
    kv_ref[:ROWS, :] = k_ref[...]
    kv_ref[ROWS:, :] = v_ref[...]


def rates_kernel(sums_ref, delta_ref, msg_ref, own_ref):
    total = jnp.sum(sums_ref[...], axis=0)
    rate = lax.rsqrt(total / (32 * WIDTH) + EPSILON)
    own_ref[...] = rate
    msg_ref[:, :8, :] = jnp.broadcast_to(rate[None], (16, 8, WIDTH))
    msg_ref[:, 8:, :] = jnp.broadcast_to(delta_ref[...][None], (16, 8, WIDTH))


def totals_kernel(
    place_ref, order_ref, rates_ref, qgain_ref, kgain_ref,
    qg0, qg1, qg2, qg3, kv0, kv1, kv2, kv3,
    total_ref, qn_ref, kn_ref,
):
    y = place_ref[0]
    x = place_ref[1]
    q_gain = qgain_ref[...].astype(F32)
    k_gain = kgain_ref[...].astype(F32)
    for d, (qg, kv) in enumerate(zip((qg0, qg1, qg2, qg3), (kv0, kv1, kv2, kv3))):
        xs = lax.rem(x - d + SIDE, SIDE)
        ys = lax.rem(y - d + SIDE, SIDE)
        q_rate = rates_ref[y * SIDE + xs]
        k_rate = rates_ref[ys * SIDE + x]
        for i in range(PIECES):
            rows = pl.ds(i * WIDTH, WIDTH)
            q = qg[rows, :].astype(F32) * column(q_rate[i : i + 1, :]) * q_gain
            k = kv[rows, :].astype(F32) * column(k_rate[PIECES + i : PIECES + i + 1, :]) * k_gain
            qn_ref[xs, rows, :] = q.astype(BF16)
            kn_ref[ys, rows, :] = k.astype(BF16)
    total_ref[...] = jnp.zeros_like(total_ref)

    def tile(t, carry):
        i = t // SIDE
        j = lax.rem(t, SIDE)

        @pl.when(order_ref[j * SIDE + x] <= order_ref[y * SIDE + i])
        def _():
            scores = dot(kn_ref[j], qn_ref[i], NT)
            total_ref[i] += jnp.sum(jnp.exp2(scores * (ROOT * LOG2E)), axis=0, keepdims=True)

        return carry

    lax.fori_loop(0, SIDE * SIDE, tile, 0)


def grads_kernel(
    place_ref, order_ref, rates_ref, total_ref, qn_ref, kn_ref,
    qg0, qg1, qg2, qg3, kv0, kv1, kv2, kv3,
    own_ref, dq1_ref, dq2_ref, dq3_ref, dkv_ref,
    dq_acc, dk_acc, dv_acc, g_all, v_all, log_all, delta_all,
):
    y = place_ref[0]
    x = place_ref[1]
    for d, (qg, kv) in enumerate(zip((qg0, qg1, qg2, qg3), (kv0, kv1, kv2, kv3))):
        xs = lax.rem(x - d + SIDE, SIDE)
        ys = lax.rem(y - d + SIDE, SIDE)
        g_all[xs] = qg[ROWS:, :]
        v_all[ys] = kv[ROWS:, :]
        stats = rates_ref[y * SIDE + xs]
        delta_all[xs] = jnp.concatenate([stats[8 + i : 9 + i, :] for i in range(PIECES)], axis=1)
    log_all[...] = jnp.log2(total_ref[...])
    dq_acc[...] = jnp.zeros_like(dq_acc)

    def key_block(j, carry):
        dk_acc[...] = jnp.zeros_like(dk_acc)
        dv_acc[...] = jnp.zeros_like(dv_acc)

        def query_block(i, inner):
            @pl.when(order_ref[j * SIDE + x] <= order_ref[y * SIDE + i])
            def _():
                keys = kn_ref[j]
                queries = qn_ref[i]
                grad = g_all[i]
                scores = dot(keys, queries, NT)
                probs = jnp.exp2(scores * (ROOT * LOG2E) - log_all[i])
                dprobs = dot(v_all[j], grad, NT)
                dscores = (probs * (dprobs - delta_all[i])).astype(BF16)
                dv_acc[...] += dot(probs.astype(BF16), grad)
                dk_acc[...] += dot(dscores, queries)
                dq_acc[i] += dot(dscores, keys, TN)

            return inner

        lax.fori_loop(0, SIDE, query_block, 0)
        dkv_ref[j, :ROWS, :] = (dk_acc[...] * ROOT).astype(BF16)
        dkv_ref[j, ROWS:, :] = dv_acc[...].astype(BF16)
        return carry

    lax.fori_loop(0, SIDE, key_block, 0)
    own_ref[...] = dq_acc[x] * ROOT
    for d, out_ref in enumerate((dq1_ref, dq2_ref, dq3_ref), 1):
        out_ref[...] = (dq_acc[lax.rem(x + d, SIDE)] * ROOT).astype(BF16)


def sums_kernel(
    own_ref, dq1_ref, dq2_ref, dq3_ref, dkv_ref, q_ref, k_ref, qgain_ref, kgain_ref,
    gq_ref, gk_ref, dv_ref, msg_ref,
):
    q_gain = qgain_ref[...].astype(F32)
    k_gain = kgain_ref[...].astype(F32)
    part = jnp.zeros((8, WIDTH), F32)
    line = lax.broadcasted_iota(jnp.int32, (8, WIDTH), 0)
    for i in range(PIECES):
        rows = pl.ds(i * WIDTH, WIDTH)
        later = pl.ds(ROWS + i * WIDTH, WIDTH)
        gq = own_ref[rows, :]
        for ref in (dq1_ref, dq2_ref, dq3_ref):
            gq = gq + ref[rows, :].astype(F32)
        gq = gq * q_gain
        gk = dkv_ref[0, rows, :].astype(F32)
        dv = dkv_ref[0, later, :].astype(F32)
        for j in range(1, SIDE):
            gk = gk + dkv_ref[j, rows, :].astype(F32)
            dv = dv + dkv_ref[j, later, :].astype(F32)
        gk = gk * k_gain
        gq_ref[rows, :] = gq
        gk_ref[rows, :] = gk
        dv_ref[rows, :] = dv.astype(BF16)
        part = jnp.where(line == i, row_sums(gq * q_ref[rows, :].astype(F32)), part)
        part = jnp.where(line == PIECES + i, row_sums(gk * k_ref[rows, :].astype(F32)), part)
    msg_ref[...] = jnp.broadcast_to(part[None], msg_ref.shape)


def final_kernel(sums_ref, own_ref, gq_ref, gk_ref, q_ref, k_ref, dq_ref, dk_ref):
    inner = jnp.sum(sums_ref[...], axis=0)
    rate = own_ref[...]
    weight = rate * rate * rate * inner / (32 * WIDTH)
    for first, g_ref, raw_ref, out_ref in ((0, gq_ref, q_ref, dq_ref), (PIECES, gk_ref, k_ref, dk_ref)):
        for i in range(PIECES):
            rows = pl.ds(i * WIDTH, WIDTH)
            line = slice(first + i, first + i + 1)
            raw = raw_ref[rows, :].astype(F32)
            out = column(rate[line, :]) * g_ref[rows, :] - raw * column(weight[line, :])
            out_ref[rows, :] = out.astype(BF16)


def local(q_raw, k_raw, values, out, d_out, q_gain, k_gain, order):
    block = struct((ROWS, WIDTH), BF16)
    wide = struct((ROWS, WIDTH), F32)
    pair = struct((2 * ROWS, WIDTH), BF16)
    message = struct((32, 8, WIDTH), F32)
    place = jnp.stack([lax.axis_index("y"), lax.axis_index("x")]).astype(jnp.int32)
    q_gain = q_gain.reshape(1, WIDTH)
    k_gain = k_gain.reshape(1, WIDTH)

    squares, delta, qg, kv = call(
        squares_kernel, (message, struct((8, WIDTH), F32), pair, pair)
    )(q_raw, k_raw, values, out, d_out)
    squares = lax.all_to_all(squares, HEAD, 0, 0)
    qgs = [qg] + [shift(qg, "x", d) for d in range(1, SIDE)]
    kvs = [kv] + [shift(kv, "y", d) for d in range(1, SIDE)]
    rates, own_rate = call(
        rates_kernel, (struct((16, 16, WIDTH), F32), struct((8, WIDTH), F32))
    )(squares, delta)
    rates = lax.all_to_all(rates, SEQ, 0, 0)

    blocks = struct((SIDE, ROWS, WIDTH), BF16)
    totals, qn, kn = call(
        totals_kernel, (struct((SIDE, 1, ROWS), F32), blocks, blocks), smem=2
    )(place, order, rates, q_gain, k_gain, *qgs, *kvs)
    totals = lax.psum(totals, "x")

    own, dq1, dq2, dq3, dkv = call(
        grads_kernel,
        (wide, block, block, block, struct((SIDE, 2 * ROWS, WIDTH), BF16)),
        scratch=(
            pltpu.VMEM((SIDE, ROWS, WIDTH), F32),
            pltpu.VMEM((ROWS, WIDTH), F32),
            pltpu.VMEM((ROWS, WIDTH), F32),
            pltpu.VMEM((SIDE, ROWS, WIDTH), BF16),
            pltpu.VMEM((SIDE, ROWS, WIDTH), BF16),
            pltpu.VMEM((SIDE, 1, ROWS), F32),
            pltpu.VMEM((SIDE, 1, ROWS), F32),
        ),
        smem=2,
    )(place, order, rates, totals, qn, kn, *qgs, *kvs)
    dkv = lax.all_to_all(dkv, "y", 0, 0)
    dq1, dq2, dq3 = (shift(part, "x", d) for d, part in enumerate((dq1, dq2, dq3), 1))

    gq, gk, dv, inner = call(sums_kernel, (wide, wide, block, message))(
        own, dq1, dq2, dq3, dkv, q_raw, k_raw, q_gain, k_gain
    )
    inner = lax.all_to_all(inner, HEAD, 0, 0)
    d_q, d_k = call(final_kernel, (block, block))(inner, own_rate, gq, gk, q_raw, k_raw)
    return d_q, d_k, dv


def solution(mesh):
    fine = Mesh(mesh.devices.reshape(SIDE, SIDE, 16, 2), ("y", "x", "z", "c"))
    both = P(SEQ, HEAD)
    return jax.shard_map(
        local,
        mesh=fine,
        in_specs=(both,) * 5 + (P(HEAD), P(HEAD), P()),
        out_specs=(both,) * 3,
        check_vma=False,
    )
```

```python
import math

import jax
import jax.numpy as jnp
from jax import lax
from jax.experimental import pallas as pl
from jax.experimental.pallas import tpu as pltpu
from jax.sharding import Mesh, PartitionSpec as P

EPSILON = 1e-06
SIDE = 4
ROWS = 384
WIDTH = 128
PIECES = ROWS // WIDTH
HEAD = ("z", "c")
SEQ = ("y", "x")
F32 = jnp.float32
BF16 = jnp.bfloat16
ROOT = WIDTH ** (-0.5)
LOG2E = math.log2(math.e)


def swap(value, axis, mask):
    return lax.ppermute(value, axis, [(i, i ^ mask) for i in range(SIDE)])


def struct(shape, dtype):
    return jax.ShapeDtypeStruct(shape, dtype)


def call(kernel, out_shape, scratch=(), spaces=None, limit=32):
    def run(*args):
        places = {"s": pltpu.SMEM, "a": pl.ANY, "v": pltpu.VMEM}
        specs = [
            pl.BlockSpec(memory_space=places[letter])
            for letter in (spaces or "").ljust(len(args), "v")
        ]
        return pl.pallas_call(
            kernel,
            out_shape=out_shape,
            in_specs=specs,
            out_specs=jax.tree.map(lambda _: pl.BlockSpec(memory_space=pltpu.VMEM), out_shape),
            scratch_shapes=scratch,
            compiler_params=pltpu.CompilerParams(vmem_limit_bytes=limit * 2**20),
        )(*args)

    return run


def column(row):
    return jnp.broadcast_to(row, (WIDTH, WIDTH)).T


def row_sums(block):
    return jnp.sum(block.T, axis=0, keepdims=True)


def dot(a, b, dims=(((1,), (0,)), ((), ()))):
    return lax.dot_general(a, b, dims, preferred_element_type=F32)


NT = (((1,), (1,)), ((), ()))
TN = (((0,), (0,)), ((), ()))


def squares_kernel(q_ref, k_ref, v_ref, g_ref, msg_ref, qg_ref, kv_ref, sems):
    first, second = pl.ds(0, ROWS), pl.ds(ROWS, ROWS)
    copies = [
        pltpu.make_async_copy(source, target, sems.at[i])
        for i, (source, target) in enumerate((
            (q_ref, qg_ref.at[first, :]),
            (k_ref, kv_ref.at[first, :]),
            (g_ref, qg_ref.at[second, :]),
            (v_ref, kv_ref.at[second, :]),
        ))
    ]
    for copy in copies:
        copy.start()
    parts = []
    for copy, ref in zip(copies[:2], (qg_ref, kv_ref)):
        copy.wait()
        for i in range(PIECES):
            block = ref[pl.ds(i * WIDTH, WIDTH), :].astype(F32)
            parts.append(row_sums(block * block))
    part = jnp.concatenate(parts, axis=1)
    for h in range(32):
        msg_ref[h] = part
    for copy in copies[2:]:
        copy.wait()


def delta_kernel(out_ref, qg_ref, qgain_ref, kgain_ref, delta_ref, qscale_ref, kscale_ref):
    delta = jnp.zeros((8, WIDTH), F32)
    line = lax.broadcasted_iota(jnp.int32, (8, WIDTH), 0)
    for i in range(PIECES):
        o = out_ref[pl.ds(i * WIDTH, WIDTH), :].astype(F32)
        g = qg_ref[pl.ds(ROWS + i * WIDTH, WIDTH), :].astype(F32)
        delta = jnp.where(line == i, row_sums(g * o), delta)
    delta_ref[...] = delta
    qscale_ref[...] = qgain_ref[...].astype(F32)
    kscale_ref[...] = kgain_ref[...].astype(F32)


def rates_kernel(sums_ref, delta_ref, msg_ref, own_ref):
    total = sums_ref[0]
    for h in range(1, 32):
        total = total + sums_ref[h]
    rate = lax.rsqrt(total / (32 * WIDTH) + EPSILON)
    line = lax.broadcasted_iota(jnp.int32, (8, WIDTH), 0)
    lines = jnp.zeros((8, WIDTH), F32)
    for i in range(2 * PIECES):
        lines = jnp.where(line == i, rate[:, i * WIDTH : (i + 1) * WIDTH], lines)
    own_ref[...] = lines
    msg_ref[:, :8, :] = jnp.broadcast_to(lines[None], (16, 8, WIDTH))
    msg_ref[:, 8:, :] = jnp.broadcast_to(delta_ref[...][None], (16, 8, WIDTH))


def totals_kernel(
    place_ref, order_hbm, rates_ref, qgain_ref, kgain_ref,
    qg0, qg1, qg2, qg3, kv0, kv1, kv2, kv3,
    total_ref, qn_ref, kn_ref, order_ref, sem,
):
    fetch = pltpu.make_async_copy(order_hbm, order_ref, sem)
    fetch.start()
    y = place_ref[0]
    x = place_ref[1]
    q_gain = qgain_ref[...]
    k_gain = kgain_ref[...]
    for d, (qg, kv) in enumerate(zip((qg0, qg1, qg2, qg3), (kv0, kv1, kv2, kv3))):
        xs = x ^ d
        ys = y ^ d
        q_rate = rates_ref[y * SIDE + xs]
        k_rate = rates_ref[ys * SIDE + x]
        for i in range(PIECES):
            rows = pl.ds(i * WIDTH, WIDTH)
            q = qg[rows, :].astype(F32) * column(q_rate[i : i + 1, :]) * q_gain
            k = kv[rows, :].astype(F32) * column(k_rate[PIECES + i : PIECES + i + 1, :]) * k_gain
            qn_ref[xs, rows, :] = q.astype(BF16)
            kn_ref[ys, rows, :] = k.astype(BF16)
    total_ref[...] = jnp.zeros_like(total_ref)
    fetch.wait()

    def tile(t, carry):
        i = t // SIDE
        j = lax.rem(t, SIDE)

        @pl.when(order_ref[j * SIDE + x] <= order_ref[y * SIDE + i])
        def _():
            scores = dot(kn_ref[j], qn_ref[i], NT)
            total_ref[i] += jnp.sum(jnp.exp2(scores * (ROOT * LOG2E)), axis=0, keepdims=True)

        return carry

    lax.fori_loop(0, SIDE * SIDE, tile, 0)


def grads_kernel(
    place_ref, order_hbm, rates_ref, qgain_ref, kgain_ref, total_ref, qn_ref, kn_ref,
    qg0, qg1, qg2, qg3, kv0, kv1, kv2, kv3,
    msg_ref, dq0_ref, dq1_ref, dq2_ref, dq3_ref, dkv0_ref, dkv1_ref, dkv2_ref, dkv3_ref,
    dq_acc, dk_acc, dv_acc, g_all, v_all, log_all, delta_all, order_ref, sem,
):
    fetch = pltpu.make_async_copy(order_hbm, order_ref, sem)
    fetch.start()
    y = place_ref[0]
    x = place_ref[1]
    for d, (qg, kv) in enumerate(zip((qg0, qg1, qg2, qg3), (kv0, kv1, kv2, kv3))):
        xs = x ^ d
        ys = y ^ d
        g_all[xs] = qg[ROWS:, :]
        v_all[ys] = kv[ROWS:, :]
        stats = rates_ref[y * SIDE + xs]
        delta_all[xs] = jnp.concatenate([stats[8 + i : 9 + i, :] for i in range(PIECES)], axis=1)
    log_all[...] = jnp.log2(total_ref[...])
    dq_acc[...] = jnp.zeros_like(dq_acc)
    dk_acc[...] = jnp.zeros_like(dk_acc)
    dv_acc[...] = jnp.zeros_like(dv_acc)
    msg_ref[...] = jnp.zeros_like(msg_ref)
    fetch.wait()

    def tile(t, carry):
        i = t // SIDE
        j = lax.rem(t, SIDE)

        @pl.when(order_ref[j * SIDE + x] <= order_ref[y * SIDE + i])
        def _():
            keys = kn_ref[j]
            queries = qn_ref[i]
            grad = g_all[i]
            scores = dot(keys, queries, NT)
            probs = jnp.exp2(scores * (ROOT * LOG2E) - log_all[i])
            dprobs = dot(v_all[j], grad, NT)
            dscores = (probs * (dprobs - delta_all[i])).astype(BF16)
            dv_acc[j] += dot(probs.astype(BF16), grad)
            dk_acc[j] += dot(dscores, queries)
            dq_acc[i] += dot(dscores, keys, TN)

        return carry

    lax.fori_loop(0, SIDE * SIDE, tile, 0)
    q_gain = qgain_ref[...] * ROOT
    k_gain = kgain_ref[...] * ROOT
    q_parts = (dq0_ref, dq1_ref, dq2_ref, dq3_ref)
    k_parts = (dkv0_ref, dkv1_ref, dkv2_ref, dkv3_ref)
    line = lax.broadcasted_iota(jnp.int32, (8, WIDTH), 0)
    for d, (qg, kv) in enumerate(zip((qg0, qg1, qg2, qg3), (kv0, kv1, kv2, kv3))):
        xs = x ^ d
        ys = y ^ d
        q_lines = jnp.zeros((8, WIDTH), F32)
        k_lines = jnp.zeros((8, WIDTH), F32)
        for i in range(PIECES):
            rows = pl.ds(i * WIDTH, WIDTH)
            later = pl.ds(ROWS + i * WIDTH, WIDTH)
            gq = dq_acc[xs, rows, :] * q_gain
            gk = dk_acc[ys, rows, :] * k_gain
            q_lines = jnp.where(line == i, row_sums(gq * qg[rows, :].astype(F32)), q_lines)
            k_lines = jnp.where(line == PIECES + i, row_sums(gk * kv[rows, :].astype(F32)), k_lines)
            q_parts[d][rows, :] = gq.astype(q_parts[d].dtype)
            k_parts[d][rows, :] = gk.astype(k_parts[d].dtype)
            k_parts[d][later, :] = dv_acc[ys, rows, :].astype(k_parts[d].dtype)
        msg_ref[y * SIDE + xs] = q_lines
        msg_ref[ys * SIDE + x] = k_lines + jnp.where(d == 0, q_lines, jnp.zeros_like(q_lines))


def inner_kernel(place_ref, sums_ref, dq1_ref, dq2_ref, dq3_ref, msg_ref, out1_ref, out2_ref, out3_ref):
    y = place_ref[0]
    x = place_ref[1]
    own = sums_ref[y * SIDE + x]
    q_lines = own
    k_lines = own
    for d in range(1, SIDE):
        q_lines = q_lines + sums_ref[y * SIDE + (x ^ d)]
        k_lines = k_lines + sums_ref[(y ^ d) * SIDE + x]
    line = lax.broadcasted_iota(jnp.int32, (8, WIDTH), 0)
    total = jnp.where(line < PIECES, q_lines, k_lines).astype(BF16)
    msg_ref[...] = jnp.broadcast_to(total[None], msg_ref.shape)
    out1_ref[...] = dq1_ref[...]
    out2_ref[...] = dq2_ref[...]
    out3_ref[...] = dq3_ref[...]


def final_kernel(
    sums_ref, own_ref, qg_ref, kv_ref,
    dq0_ref, dq1_ref, dq2_ref, dq3_ref, dkv0_ref, dkv1_ref, dkv2_ref, dkv3_ref,
    dq_ref, dk_ref, dv_ref,
):
    inner = jnp.sum(sums_ref[...].astype(F32), axis=0)
    rate = own_ref[...]
    weight = rate * rate * rate * inner / (32 * WIDTH)

    def total(refs, rows):
        value = refs[0][rows, :]
        for ref in refs[1:]:
            value = value + ref[rows, :].astype(F32)
        return value

    q_parts = (dq0_ref, dq1_ref, dq2_ref, dq3_ref)
    k_parts = (dkv0_ref, dkv1_ref, dkv2_ref, dkv3_ref)
    for i in range(PIECES):
        rows = pl.ds(i * WIDTH, WIDTH)
        later = pl.ds(ROWS + i * WIDTH, WIDTH)
        for first, parts, raw_ref, out_ref in ((0, q_parts, qg_ref, dq_ref), (PIECES, k_parts, kv_ref, dk_ref)):
            line = slice(first + i, first + i + 1)
            raw = raw_ref[rows, :].astype(F32)
            out = column(rate[line, :]) * total(parts, rows) - raw * column(weight[line, :])
            out_ref[rows, :] = out.astype(BF16)
        dv_ref[rows, :] = total(k_parts, later).astype(BF16)


def local(q_raw, k_raw, values, out, d_out, q_gain, k_gain, order):
    block = struct((ROWS, WIDTH), BF16)
    pair = struct((2 * ROWS, WIDTH), BF16)
    lines = struct((8, WIDTH), F32)
    gain = struct((1, WIDTH), F32)
    place = jnp.stack([lax.axis_index("y"), lax.axis_index("x")]).astype(jnp.int32)

    squares, qg, kv = call(
        squares_kernel,
        (struct((32, 1, 2 * ROWS), F32), pair, pair),
        scratch=(pltpu.SemaphoreType.DMA((4,)),),
        spaces="aaaa",
    )(q_raw, k_raw, values, d_out)
    squares = lax.all_to_all(squares, HEAD, 0, 0)
    qgs = [qg] + [swap(qg, "x", d) for d in range(1, SIDE)]
    kvs = [kv] + [swap(kv, "y", d) for d in range(1, SIDE)]
    delta, q_scale, k_scale = call(delta_kernel, (lines, gain, gain))(
        out, qg, q_gain.reshape(1, WIDTH), k_gain.reshape(1, WIDTH)
    )
    rates, own_rate = call(rates_kernel, (struct((16, 16, WIDTH), F32), lines))(squares, delta)
    rates = lax.all_to_all(rates, SEQ, 0, 0)

    blocks = struct((SIDE, ROWS, WIDTH), BF16)
    known = (pltpu.SMEM((16,), jnp.int32), pltpu.SemaphoreType.DMA)
    totals, qn, kn = call(
        totals_kernel,
        (struct((SIDE, 1, ROWS), F32), blocks, blocks),
        scratch=known,
        spaces="sa",
    )(place, order, rates, q_scale, k_scale, *qgs, *kvs)
    totals = lax.psum(totals, "x")

    own = (struct((ROWS, WIDTH), F32), block, block, block)
    own_pair = (struct((2 * ROWS, WIDTH), F32), pair, pair, pair)
    inner, *parts = call(
        grads_kernel,
        (struct((16, 8, WIDTH), F32),) + own + own_pair,
        scratch=(
            pltpu.VMEM((SIDE, ROWS, WIDTH), F32),
            pltpu.VMEM((SIDE, ROWS, WIDTH), F32),
            pltpu.VMEM((SIDE, ROWS, WIDTH), F32),
            pltpu.VMEM((SIDE, ROWS, WIDTH), BF16),
            pltpu.VMEM((SIDE, ROWS, WIDTH), BF16),
            pltpu.VMEM((SIDE, 1, ROWS), F32),
            pltpu.VMEM((SIDE, 1, ROWS), F32),
        ) + known,
        spaces="sa",
    )(place, order, rates, q_scale, k_scale, totals, qn, kn, *qgs, *kvs)
    dqs, dkvs = parts[:SIDE], parts[SIDE:]
    inner = lax.all_to_all(inner, SEQ, 0, 0)
    dkvs[1:] = [swap(part, "y", d) for d, part in enumerate(dkvs[1:], 1)]
    inner, *dqs[1:] = call(
        inner_kernel, (struct((32, 8, WIDTH), BF16), block, block, block), spaces="s"
    )(place, inner, *dqs[1:])
    inner = lax.all_to_all(inner, HEAD, 0, 0)
    dqs[1:] = [swap(part, "x", d) for d, part in enumerate(dqs[1:], 1)]
    return call(final_kernel, (block, block, block))(inner, own_rate, qg, kv, *dqs, *dkvs)


def solution(mesh):
    fine = Mesh(mesh.devices.reshape(SIDE, SIDE, 16, 2), ("y", "x", "z", "c"))
    both = P(SEQ, HEAD)
    return jax.shard_map(
        local,
        mesh=fine,
        in_specs=(both,) * 5 + (P(HEAD), P(HEAD), P()),
        out_specs=(both,) * 3,
        check_vma=False,
    )
```

```python
import math

import jax
import jax.numpy as jnp
from jax import lax
from jax.experimental import pallas as pl
from jax.experimental.pallas import tpu as pltpu
from jax.sharding import Mesh, PartitionSpec as P

EPSILON = 1e-06
SIDE = 4
HEADS = 32
ROWS = 384
WIDTH = 128
PIECES = ROWS // WIDTH
LINES = 16
HEAD = ("z", "c")
SEQ = ("y", "x")
F32 = jnp.float32
BF16 = jnp.bfloat16
ROOT = WIDTH ** (-0.5)
LOG2E = math.log2(math.e)
NT = (((1,), (1,)), ((), ()))
TN = (((0,), (0,)), ((), ()))


def swap(value, axis, mask):
    return lax.ppermute(value, axis, [(i, i ^ mask) for i in range(SIDE)])


def struct(shape, dtype):
    return jax.ShapeDtypeStruct(shape, dtype)


def call(kernel, out_shape, scratch=(), spaces="", limit=32):
    def run(*args):
        places = {"s": pltpu.SMEM, "h": pltpu.HBM, "v": pltpu.VMEM}
        specs = [pl.BlockSpec(memory_space=places[s]) for s in spaces.ljust(len(args), "v")]
        return pl.pallas_call(
            kernel,
            out_shape=out_shape,
            in_specs=specs,
            out_specs=jax.tree.map(lambda _: pl.BlockSpec(memory_space=pltpu.VMEM), out_shape),
            scratch_shapes=scratch,
            compiler_params=pltpu.CompilerParams(vmem_limit_bytes=limit * 2**20),
        )(*args)

    return run


def column(row):
    return jnp.broadcast_to(row, (WIDTH, WIDTH)).T


def row_sums(block):
    return jnp.sum(block.T, axis=0, keepdims=True)


def dot(a, b, dims=(((1,), (0,)), ((), ()))):
    return lax.dot_general(a, b, dims, preferred_element_type=F32)


def squares_kernel(q_hbm, k_hbm, msg_ref, q_ref, k_ref, sems):
    copies = [
        pltpu.make_async_copy(source, target, sems.at[i])
        for i, (source, target) in enumerate(((q_hbm, q_ref), (k_hbm, k_ref)))
    ]
    for copy in copies:
        copy.start()
    parts = []
    for copy, ref in zip(copies, (q_ref, k_ref)):
        copy.wait()
        for i in range(PIECES):
            block = ref[pl.ds(i * WIDTH, WIDTH), :].astype(F32)
            parts.append(row_sums(block * block))
    part = jnp.concatenate(parts, axis=1)
    for h in range(HEADS):
        msg_ref[h] = part


def delta_kernel(out_ref, grad_ref, qgain_ref, kgain_ref, delta_ref, qscale_ref, kscale_ref):
    line = lax.broadcasted_iota(jnp.int32, (LINES, WIDTH), 0)
    lines = jnp.zeros((LINES, WIDTH), F32)
    for i in range(PIECES):
        rows = pl.ds(i * WIDTH, WIDTH)
        delta = row_sums(out_ref[rows, :].astype(F32) * grad_ref[rows, :].astype(F32))
        high = delta.astype(BF16).astype(F32)
        lines = jnp.where(line == i, high, lines)
        lines = jnp.where(line == PIECES + i, delta - high, lines)
    delta_ref[...] = lines.astype(BF16)
    qscale_ref[...] = qgain_ref[...].astype(F32)
    kscale_ref[...] = kgain_ref[...].astype(F32)


def norms_kernel(
    sums_ref, q_ref, k_ref, grad_ref, values_ref, delta_ref, qscale_ref, kscale_ref,
    rate_ref, qmsg_ref, kmsg_ref,
):
    total = sums_ref[0]
    for h in range(1, HEADS):
        total = total + sums_ref[h]
    rate = lax.rsqrt(total / (HEADS * WIDTH) + EPSILON)
    line = lax.broadcasted_iota(jnp.int32, (8, WIDTH), 0)
    lines = jnp.zeros((8, WIDTH), F32)
    for i in range(2 * PIECES):
        lines = jnp.where(line == i, rate[:, i * WIDTH : (i + 1) * WIDTH], lines)
    rate_ref[...] = lines
    for i in range(PIECES):
        rows = pl.ds(i * WIDTH, WIDTH)
        later = pl.ds(ROWS + i * WIDTH, WIDTH)
        q = q_ref[rows, :].astype(F32) * column(lines[i : i + 1, :]) * qscale_ref[...]
        k = k_ref[rows, :].astype(F32) * column(lines[PIECES + i : PIECES + i + 1, :]) * kscale_ref[...]
        q = q.astype(BF16)
        for x in range(SIDE):
            qmsg_ref[x, rows, :] = q
            qmsg_ref[x, later, :] = grad_ref[rows, :]
        kmsg_ref[rows, :] = k.astype(BF16)
        kmsg_ref[later, :] = values_ref[rows, :]
    for x in range(SIDE):
        qmsg_ref[x, 2 * ROWS :, :] = delta_ref[...]


def totals_kernel(place_ref, order_hbm, qall_ref, kall_ref, total_ref, order_ref, sem):
    fetch = pltpu.make_async_copy(order_hbm, order_ref, sem)
    fetch.start()
    y = place_ref[0]
    x = place_ref[1]
    total_ref[...] = jnp.zeros_like(total_ref)
    fetch.wait()

    def tile(t, carry):
        j = t // SIDE
        i = lax.rem(t, SIDE)

        @pl.when(order_ref[j * SIDE + x] <= order_ref[y * SIDE + i])
        def _():
            scores = dot(kall_ref[j, :ROWS, :], qall_ref[i, :ROWS, :], NT)
            total_ref[i] += jnp.sum(jnp.exp2(scores * (ROOT * LOG2E)), axis=0, keepdims=True)

        return carry

    lax.fori_loop(0, SIDE * SIDE, tile, 0)


def grads_kernel(
    place_ref, order_hbm, total_ref, qall_ref, kall_ref,
    dkv_ref, dq0_ref, dq1_ref, dq2_ref, dq3_ref,
    dq_acc, dk_acc, dv_acc, log_all, delta_all, order_ref, sem,
):
    fetch = pltpu.make_async_copy(order_hbm, order_ref, sem)
    fetch.start()
    y = place_ref[0]
    x = place_ref[1]
    log_all[...] = jnp.log2(total_ref[...])
    for i in range(SIDE):
        lines = qall_ref[i, 2 * ROWS :, :].astype(F32)
        high = jnp.concatenate([lines[p : p + 1, :] for p in range(PIECES)], axis=1)
        low = jnp.concatenate([lines[PIECES + p : PIECES + p + 1, :] for p in range(PIECES)], axis=1)
        delta_all[i] = high + low
    dq_acc[...] = jnp.zeros_like(dq_acc)
    dk_acc[...] = jnp.zeros_like(dk_acc)
    dv_acc[...] = jnp.zeros_like(dv_acc)
    fetch.wait()

    def tile(t, carry):
        j = t // SIDE
        i = lax.rem(t, SIDE)

        @pl.when(order_ref[j * SIDE + x] <= order_ref[y * SIDE + i])
        def _():
            keys = kall_ref[j, :ROWS, :]
            queries = qall_ref[i, :ROWS, :]
            grad = qall_ref[i, ROWS : 2 * ROWS, :]
            scores = dot(keys, queries, NT)
            probs = jnp.exp2(scores * (ROOT * LOG2E) - log_all[i])
            dprobs = dot(kall_ref[j, ROWS:, :], grad, NT)
            dscores = (probs * (dprobs - delta_all[i])).astype(BF16)
            dv_acc[j] += dot(probs.astype(BF16), grad)
            dk_acc[j] += dot(dscores, queries)
            dq_acc[i] += dot(dscores, keys, TN)

        return carry

    lax.fori_loop(0, SIDE * SIDE, tile, 0)
    dkv_ref[:, :ROWS, :] = (dk_acc[...] * ROOT).astype(BF16)
    dkv_ref[:, ROWS:, :] = dv_acc[...].astype(BF16)
    for d, ref in enumerate((dq0_ref, dq1_ref, dq2_ref, dq3_ref)):
        ref[...] = (dq_acc[x ^ d] * ROOT).astype(BF16)


def sums_kernel(
    dkv_ref, dq0_ref, dq1_ref, dq2_ref, dq3_ref, q_ref, k_ref, qscale_ref, kscale_ref,
    gq_ref, gk_ref, dv_ref, msg_ref,
):
    parts = (dq0_ref, dq1_ref, dq2_ref, dq3_ref)
    line = lax.broadcasted_iota(jnp.int32, (8, WIDTH), 0)
    lines = jnp.zeros((8, WIDTH), F32)
    for i in range(PIECES):
        rows = pl.ds(i * WIDTH, WIDTH)
        later = pl.ds(ROWS + i * WIDTH, WIDTH)
        gq = sum(part[rows, :].astype(F32) for part in parts) * qscale_ref[...]
        gk = sum(dkv_ref[j, rows, :].astype(F32) for j in range(SIDE)) * kscale_ref[...]
        gq_ref[rows, :] = gq
        gk_ref[rows, :] = gk
        dv_ref[rows, :] = sum(dkv_ref[j, later, :].astype(F32) for j in range(SIDE)).astype(BF16)
        lines = jnp.where(line == i, row_sums(gq * q_ref[rows, :].astype(F32)), lines)
        lines = jnp.where(line == PIECES + i, row_sums(gk * k_ref[rows, :].astype(F32)), lines)
    msg_ref[...] = jnp.broadcast_to(lines.astype(BF16)[None], msg_ref.shape)


def final_kernel(sums_ref, rate_ref, gq_ref, gk_ref, q_ref, k_ref, dq_ref, dk_ref):
    inner = jnp.sum(sums_ref[...].astype(F32), axis=0)
    rate = rate_ref[...]
    weight = rate * rate * rate * inner / (HEADS * WIDTH)
    for first, g_ref, raw_ref, out_ref in ((0, gq_ref, q_ref, dq_ref), (PIECES, gk_ref, k_ref, dk_ref)):
        for i in range(PIECES):
            rows = pl.ds(i * WIDTH, WIDTH)
            line = slice(first + i, first + i + 1)
            raw = raw_ref[rows, :].astype(F32)
            out = column(rate[line, :]) * g_ref[rows, :] - raw * column(weight[line, :])
            out_ref[rows, :] = out.astype(BF16)


def local(q_raw, k_raw, values, out, d_out, q_gain, k_gain, order):
    block = struct((ROWS, WIDTH), BF16)
    wide = struct((ROWS, WIDTH), F32)
    pair = struct((2 * ROWS, WIDTH), BF16)
    lines = struct((8, WIDTH), F32)
    gain = struct((1, WIDTH), F32)
    known = (pltpu.SMEM((16,), jnp.int32), pltpu.SemaphoreType.DMA)
    place = jnp.stack([lax.axis_index("y"), lax.axis_index("x")]).astype(jnp.int32)

    squares, q_raw, k_raw = call(
        squares_kernel,
        (struct((HEADS, 1, 2 * ROWS), F32), block, block),
        scratch=(pltpu.SemaphoreType.DMA((2,)),),
        spaces="hh",
        limit=60,
    )(q_raw, k_raw)
    squares = lax.all_to_all(squares, HEAD, 0, 0)
    delta, q_scale, k_scale = call(delta_kernel, (struct((LINES, WIDTH), BF16), gain, gain))(
        out, d_out, q_gain.reshape(1, WIDTH), k_gain.reshape(1, WIDTH)
    )
    rate, queries, keys = call(
        norms_kernel, (lines, struct((SIDE, 2 * ROWS + LINES, WIDTH), BF16), pair)
    )(squares, q_raw, k_raw, d_out, values, delta, q_scale, k_scale)
    queries = lax.all_to_all(queries, "x", 0, 0)
    keys = lax.all_gather(keys, "y", axis=0, tiled=True).reshape(SIDE, 2 * ROWS, WIDTH)

    totals = call(
        totals_kernel, struct((SIDE, 1, ROWS), F32), scratch=known, spaces="sh"
    )(place, order, queries, keys)
    totals = lax.psum(totals, "x")

    keys, *queries = call(
        grads_kernel,
        (struct((SIDE, 2 * ROWS, WIDTH), BF16), block, block, block, block),
        scratch=(
            pltpu.VMEM((SIDE, ROWS, WIDTH), F32),
            pltpu.VMEM((SIDE, ROWS, WIDTH), F32),
            pltpu.VMEM((SIDE, ROWS, WIDTH), F32),
            pltpu.VMEM((SIDE, 1, ROWS), F32),
            pltpu.VMEM((SIDE, 1, ROWS), F32),
        ) + known,
        spaces="sh",
    )(place, order, totals, queries, keys)
    keys = lax.all_to_all(keys, "y", 0, 0)
    queries[1:] = [swap(part, "x", d) for d, part in enumerate(queries[1:], 1)]

    gq, gk, dv, inner = call(
        sums_kernel, (wide, wide, block, struct((HEADS, 8, WIDTH), BF16))
    )(keys, *queries, q_raw, k_raw, q_scale, k_scale)
    inner = lax.all_to_all(inner, HEAD, 0, 0)
    d_q, d_k = call(final_kernel, (block, block))(inner, rate, gq, gk, q_raw, k_raw)
    return d_q, d_k, dv


def solution(mesh):
    fine = Mesh(mesh.devices.reshape(SIDE, SIDE, 16, 2), ("y", "x", "z", "c"))
    both = P(SEQ, HEAD)
    return jax.shard_map(
        local,
        mesh=fine,
        in_specs=(both,) * 5 + (P(HEAD), P(HEAD), P()),
        out_specs=(both,) * 3,
        check_vma=False,
    )
```

```python
import math

import jax
import jax.numpy as jnp
from jax import lax
from jax.experimental import pallas as pl
from jax.experimental.pallas import tpu as pltpu
from jax.sharding import Mesh, PartitionSpec as P

EPSILON = 1e-06
SIDE = 4
HEADS = 32
ROWS = 384
WIDTH = 128
PIECES = ROWS // WIDTH
LINES = 16
HEAD = ("z", "c")
SEQ = ("y", "x")
F32 = jnp.float32
BF16 = jnp.bfloat16
ROOT = WIDTH ** (-0.5)
LOG2E = math.log2(math.e)
NT = (((1,), (1,)), ((), ()))
TN = (((0,), (0,)), ((), ()))


def swap(value, axis, mask):
    return lax.ppermute(value, axis, [(i, i ^ mask) for i in range(SIDE)])


def struct(shape, dtype):
    return jax.ShapeDtypeStruct(shape, dtype)


def call(kernel, out_shape, scratch=(), spaces="", limit=32):
    def run(*args):
        memory = {"s": pltpu.SMEM, "v": pltpu.VMEM}
        specs = [pl.BlockSpec(memory_space=memory[s]) for s in spaces.ljust(len(args), "v")]
        return pl.pallas_call(
            kernel,
            out_shape=out_shape,
            in_specs=specs,
            out_specs=jax.tree.map(lambda _: pl.BlockSpec(memory_space=pltpu.VMEM), out_shape),
            scratch_shapes=scratch,
            compiler_params=pltpu.CompilerParams(vmem_limit_bytes=limit * 2**20),
        )(*args)

    return run


def column(row):
    return jnp.broadcast_to(row, (WIDTH, WIDTH)).T


def row_sums(block):
    return jnp.sum(block.T, axis=0, keepdims=True)


def dot(a, b, dims=(((1,), (0,)), ((), ()))):
    return lax.dot_general(a, b, dims, preferred_element_type=F32)


def squares_kernel(q_ref, k_ref, msg_ref):
    sums = []
    for ref in (q_ref, k_ref):
        parts = []
        for i in range(PIECES):
            block = ref[pl.ds(i * WIDTH, WIDTH), :].astype(F32)
            parts.append(row_sums(block * block))
        sums.append(jnp.concatenate(parts, axis=1))
    both = jnp.concatenate(sums, axis=0)
    square = both * both
    coded = (square * square).astype(BF16)
    for h in range(HEADS):
        msg_ref[h] = coded


def ready_kernel(
    place_ref, order_ref, q_ref, k_ref, g_ref, v_ref, o_ref, qgain_ref, kgain_ref,
    q_out, k_out, g_out, v_out, lines_ref, qscale_ref, kscale_ref,
):
    group = order_ref[place_ref[0] * SIDE + place_ref[1]].astype(F32)
    line = lax.broadcasted_iota(jnp.int32, (LINES, WIDTH), 0)
    lines = jnp.full((LINES, WIDTH), group, F32)
    for i in range(PIECES):
        rows = pl.ds(i * WIDTH, WIDTH)
        delta = row_sums(o_ref[rows, :].astype(F32) * g_ref[rows, :].astype(F32))
        high = delta.astype(BF16).astype(F32)
        lines = jnp.where(line == i, high, lines)
        lines = jnp.where(line == PIECES + i, delta - high, lines)
    lines_ref[...] = lines.astype(BF16)
    for source, target in ((q_ref, q_out), (k_ref, k_out), (g_ref, g_out), (v_ref, v_out)):
        target[...] = source[...]
    qscale_ref[...] = qgain_ref[...].astype(F32)
    kscale_ref[...] = kgain_ref[...].astype(F32)


def norms_kernel(
    sums_ref, q_ref, k_ref, g_ref, v_ref, lines_ref, qscale_ref, kscale_ref,
    rate_ref, qmsg_ref, kmsg_ref,
):
    total = jnp.zeros((2, ROWS), F32)
    for h in range(HEADS):
        total = total + jnp.sqrt(jnp.sqrt(jnp.maximum(sums_ref[h].astype(F32), 1e-36)))
    rate = lax.rsqrt(total / (HEADS * WIDTH) + EPSILON)
    rate_ref[...] = rate
    for i in range(PIECES):
        rows = pl.ds(i * WIDTH, WIDTH)
        later = pl.ds(ROWS + i * WIDTH, WIDTH)
        span = slice(i * WIDTH, (i + 1) * WIDTH)
        q = q_ref[rows, :].astype(F32) * column(rate[0:1, span]) * qscale_ref[...]
        k = k_ref[rows, :].astype(F32) * column(rate[1:2, span]) * kscale_ref[...]
        q = q.astype(BF16)
        for x in range(SIDE):
            qmsg_ref[x, rows, :] = q
            qmsg_ref[x, later, :] = g_ref[rows, :]
        kmsg_ref[rows, :] = k.astype(BF16)
        kmsg_ref[later, :] = v_ref[rows, :]
    for x in range(SIDE):
        qmsg_ref[x, 2 * ROWS :, :] = lines_ref[...]
    kmsg_ref[2 * ROWS :, :] = lines_ref[...]


def across(lines, first):
    return jnp.concatenate([lines[first + p : first + p + 1, :] for p in range(PIECES)], axis=1)


def query_groups(qall_ref):
    rows = [qall_ref[i, 2 * ROWS :, :].astype(F32)[2 * PIECES : 2 * PIECES + 1, :] for i in range(SIDE)]
    return jnp.concatenate([row for row in rows for _ in range(PIECES)], axis=1)


def key_group(kall_ref, j):
    row = kall_ref[j, 2 * ROWS :, :].astype(F32)[2 * PIECES : 2 * PIECES + 1, :]
    return jnp.concatenate([row] * (SIDE * PIECES), axis=1)


def totals_kernel(qall_ref, kall_ref, total_ref, q_all):
    for i in range(SIDE):
        q_all[i * ROWS : (i + 1) * ROWS, :] = qall_ref[i, :ROWS, :]
    groups = query_groups(qall_ref)

    def key_block(j, total):
        scores = dot(kall_ref[j, :ROWS, :], q_all[...], NT)
        part = jnp.sum(jnp.exp2(scores * (ROOT * LOG2E)), axis=0, keepdims=True)
        return total + jnp.where(key_group(kall_ref, j) <= groups, part, 0.0)

    total = lax.fori_loop(0, SIDE, key_block, jnp.zeros((1, SIDE * ROWS), F32))
    for i in range(SIDE):
        total_ref[i] = total[:, i * ROWS : (i + 1) * ROWS]


def grads_kernel(
    place_ref, total_ref, qall_ref, kall_ref,
    dkv_ref, dq0_ref, dq1_ref, dq2_ref, dq3_ref,
    q_all, g_all, k_all, v_all, logs, deltas, groups, dq_acc,
):
    for i in range(SIDE):
        span = slice(i * ROWS, (i + 1) * ROWS)
        q_all[span, :] = qall_ref[i, :ROWS, :]
        g_all[span, :] = qall_ref[i, ROWS : 2 * ROWS, :]
        k_all[span, :] = kall_ref[i, :ROWS, :]
        v_all[span, :] = kall_ref[i, ROWS : 2 * ROWS, :]
        lines = qall_ref[i, 2 * ROWS :, :].astype(F32)
        deltas[:, span] = across(lines, 0) + across(lines, PIECES)
        logs[:, span] = jnp.log2(total_ref[i])
    groups[...] = query_groups(qall_ref)
    dq_acc[...] = jnp.zeros_like(dq_acc)
    half = SIDE * ROWS // 2

    def key_pair(m, carry):
        rows = pl.ds(pl.multiple_of(m * half, half), half)
        keys = k_all[rows, :]
        vals = v_all[rows, :]
        shifts = [
            jnp.where(key_group(kall_ref, 2 * m + n) <= groups[...], logs[...], 1e30) for n in range(2)
        ]

        def part(h):
            span = slice(h * half, (h + 1) * half)
            queries = q_all[span, :]
            grad = g_all[span, :]
            scores = dot(keys, queries, NT) * (ROOT * LOG2E)
            upper = scores[:ROWS] - shifts[0][:, span]
            lower = scores[ROWS:] - shifts[1][:, span]
            probs = jnp.exp2(jnp.concatenate([upper, lower], axis=0))
            dprobs = dot(vals, grad, NT)
            dscores = (probs * (dprobs - deltas[:, span])).astype(BF16)
            dq_acc[:, span] += dot(keys, dscores, TN)
            return dot(dscores, queries), dot(probs.astype(BF16), grad)

        first, second = part(0), part(1)
        dk = ((first[0] + second[0]) * ROOT).astype(BF16)
        dv = (first[1] + second[1]).astype(BF16)
        for n in range(2):
            dkv_ref[2 * m + n, :ROWS, :] = dk[n * ROWS : (n + 1) * ROWS]
            dkv_ref[2 * m + n, ROWS:, :] = dv[n * ROWS : (n + 1) * ROWS]
        return carry

    lax.fori_loop(0, SIDE // 2, key_pair, 0)
    x = place_ref[1]
    for d, ref in enumerate((dq0_ref, dq1_ref, dq2_ref, dq3_ref)):
        span = pl.ds(pl.multiple_of((x ^ d) * ROWS, ROWS), ROWS)
        ref[...] = (dq_acc[:, span].T * ROOT).astype(BF16)


def sums_kernel(
    dkv_ref, dq0_ref, dq1_ref, dq2_ref, dq3_ref, q_ref, k_ref, qscale_ref, kscale_ref,
    gq_ref, gk_ref, dv_ref, msg_ref,
):
    parts = (dq0_ref, dq1_ref, dq2_ref, dq3_ref)
    q_lines = []
    k_lines = []
    for i in range(PIECES):
        rows = pl.ds(i * WIDTH, WIDTH)
        later = pl.ds(ROWS + i * WIDTH, WIDTH)
        gq = sum(part[rows, :].astype(F32) for part in parts) * qscale_ref[...]
        gk = sum(dkv_ref[j, rows, :].astype(F32) for j in range(SIDE)) * kscale_ref[...]
        gq_ref[rows, :] = gq
        gk_ref[rows, :] = gk
        dv_ref[rows, :] = sum(dkv_ref[j, later, :].astype(F32) for j in range(SIDE)).astype(BF16)
        q_lines.append(row_sums(gq * q_ref[rows, :].astype(F32)))
        k_lines.append(row_sums(gk * k_ref[rows, :].astype(F32)))
    both = [jnp.concatenate(lines, axis=1) for lines in (q_lines, k_lines)]
    coded = jnp.concatenate(both, axis=0).astype(BF16)
    for h in range(HEADS):
        msg_ref[h] = coded


def final_kernel(sums_ref, rate_ref, gq_ref, gk_ref, q_ref, k_ref, dq_ref, dk_ref):
    inner = jnp.zeros((2, ROWS), F32)
    for h in range(HEADS):
        inner = inner + sums_ref[h].astype(F32)
    rate = rate_ref[...]
    weight = rate * rate * rate * inner / (HEADS * WIDTH)
    for n, (g_ref, raw_ref, out_ref) in enumerate(((gq_ref, q_ref, dq_ref), (gk_ref, k_ref, dk_ref))):
        for i in range(PIECES):
            rows = pl.ds(i * WIDTH, WIDTH)
            span = slice(i * WIDTH, (i + 1) * WIDTH)
            raw = raw_ref[rows, :].astype(F32)
            out = column(rate[n : n + 1, span]) * g_ref[rows, :] - raw * column(weight[n : n + 1, span])
            out_ref[rows, :] = out.astype(BF16)


def local(q_raw, k_raw, values, out, d_out, q_gain, k_gain, order):
    block = struct((ROWS, WIDTH), BF16)
    wide = struct((ROWS, WIDTH), F32)
    pair = struct((2 * ROWS, WIDTH), BF16)
    message = struct((HEADS, 2, ROWS), BF16)
    place = jnp.stack([lax.axis_index("y"), lax.axis_index("x")]).astype(jnp.int32)
    q_gain = q_gain.reshape(1, WIDTH)
    k_gain = k_gain.reshape(1, WIDTH)

    squares = call(squares_kernel, message, limit=60)(q_raw, k_raw)
    squares = lax.all_to_all(squares, HEAD, 0, 0)
    gain = struct((1, WIDTH), F32)
    q_raw, k_raw, d_out, values, lines, q_gain, k_gain = call(
        ready_kernel,
        (block, block, block, block, struct((LINES, WIDTH), BF16), gain, gain),
        spaces="ss",
    )(place, order, q_raw, k_raw, d_out, values, out, q_gain, k_gain)
    rate, queries, keys = call(
        norms_kernel,
        (
            struct((2, ROWS), F32),
            struct((SIDE, 2 * ROWS + LINES, WIDTH), BF16),
            struct((2 * ROWS + LINES, WIDTH), BF16),
        ),
    )(squares, q_raw, k_raw, d_out, values, lines, q_gain, k_gain)
    queries = lax.all_to_all(queries, "x", 0, 0)
    keys = lax.all_gather(keys, "y", axis=0, tiled=True).reshape(SIDE, 2 * ROWS + LINES, WIDTH)

    totals = call(
        totals_kernel,
        struct((SIDE, 1, ROWS), F32),
        scratch=(pltpu.VMEM((SIDE * ROWS, WIDTH), BF16),),
    )(queries, keys)
    totals = lax.psum(totals, "x")

    tall = pltpu.VMEM((SIDE * ROWS, WIDTH), BF16)
    row = pltpu.VMEM((1, SIDE * ROWS), F32)
    keys, *queries = call(
        grads_kernel,
        (struct((SIDE, 2 * ROWS, WIDTH), BF16), block, block, block, block),
        scratch=(tall, tall, tall, tall, row, row, row, pltpu.VMEM((WIDTH, SIDE * ROWS), F32)),
        spaces="s",
    )(place, totals, queries, keys)
    keys = lax.all_to_all(keys, "y", 0, 0)
    queries[1:] = [swap(part, "x", d) for d, part in enumerate(queries[1:], 1)]

    gq, gk, dv, inner = call(
        sums_kernel, (wide, wide, block, message)
    )(keys, *queries, q_raw, k_raw, q_gain, k_gain)
    inner = lax.all_to_all(inner, HEAD, 0, 0)
    d_q, d_k = call(final_kernel, (block, block))(inner, rate, gq, gk, q_raw, k_raw)
    return d_q, d_k, dv


def solution(mesh):
    fine = Mesh(mesh.devices.reshape(SIDE, SIDE, 16, 2), ("y", "x", "z", "c"))
    both = P(SEQ, HEAD)
    return jax.shard_map(
        local,
        mesh=fine,
        in_specs=(both,) * 5 + (P(HEAD), P(HEAD), P()),
        out_specs=(both,) * 3,
        check_vma=False,
    )
```

```python
import math

import jax
import jax.numpy as jnp
from jax import lax
from jax.experimental import pallas as pl
from jax.experimental.pallas import tpu as pltpu
from jax.sharding import Mesh, PartitionSpec as P

EPSILON = 1e-06
SIDE = 4
HEADS = 32
ROWS = 384
WIDTH = 128
PIECES = ROWS // WIDTH
LINES = 16
HEAD = ("z", "c")
SEQ = ("y", "x")
F32 = jnp.float32
BF16 = jnp.bfloat16
ROOT = WIDTH ** (-0.5)
LOG2E = math.log2(math.e)
NT = (((1,), (1,)), ((), ()))
TN = (((0,), (0,)), ((), ()))


def swap(value, axis, mask):
    return lax.ppermute(value, axis, [(i, i ^ mask) for i in range(SIDE)])


def struct(shape, dtype):
    return jax.ShapeDtypeStruct(shape, dtype)


def call(kernel, out_shape, scratch=(), spaces="", limit=32):
    def run(*args):
        memory = {"s": pltpu.SMEM, "v": pltpu.VMEM}
        specs = [pl.BlockSpec(memory_space=memory[s]) for s in spaces.ljust(len(args), "v")]
        return pl.pallas_call(
            kernel,
            out_shape=out_shape,
            in_specs=specs,
            out_specs=jax.tree.map(lambda _: pl.BlockSpec(memory_space=pltpu.VMEM), out_shape),
            scratch_shapes=scratch,
            compiler_params=pltpu.CompilerParams(vmem_limit_bytes=limit * 2**20),
        )(*args)

    return run


def column(row):
    return jnp.broadcast_to(row, (WIDTH, WIDTH)).T


def row_sums(block):
    return jnp.sum(block.T, axis=0, keepdims=True)


def dot(a, b, dims=(((1,), (0,)), ((), ()))):
    return lax.dot_general(a, b, dims, preferred_element_type=F32)


def squares_kernel(q_ref, k_ref, msg_ref):
    sums = []
    for ref in (q_ref, k_ref):
        parts = []
        for i in range(PIECES):
            block = ref[pl.ds(i * WIDTH, WIDTH), :].astype(F32)
            parts.append(row_sums(block * block))
        sums.append(jnp.concatenate(parts, axis=1))
    both = jnp.concatenate(sums, axis=0)
    square = both * both
    coded = (square * square).astype(BF16)
    for h in range(HEADS):
        msg_ref[h] = coded


def ready_kernel(
    place_ref, order_ref, q_ref, k_ref, g_ref, v_ref, o_ref, qgain_ref, kgain_ref,
    q_out, k_out, g_out, v_out, lines_ref, qscale_ref, kscale_ref,
):
    group = order_ref[place_ref[0] * SIDE + place_ref[1]].astype(F32)
    line = lax.broadcasted_iota(jnp.int32, (LINES, WIDTH), 0)
    lines = jnp.full((LINES, WIDTH), group, F32)
    for i in range(PIECES):
        rows = pl.ds(i * WIDTH, WIDTH)
        delta = row_sums(o_ref[rows, :].astype(F32) * g_ref[rows, :].astype(F32))
        high = delta.astype(BF16).astype(F32)
        lines = jnp.where(line == i, high, lines)
        lines = jnp.where(line == PIECES + i, delta - high, lines)
    lines_ref[...] = lines.astype(BF16)
    for source, target in ((q_ref, q_out), (k_ref, k_out), (g_ref, g_out), (v_ref, v_out)):
        target[...] = source[...]
    qscale_ref[...] = qgain_ref[...].astype(F32)
    kscale_ref[...] = kgain_ref[...].astype(F32)


def norms_kernel(
    sums_ref, q_ref, k_ref, g_ref, v_ref, lines_ref, qscale_ref, kscale_ref,
    rate_ref, qmsg_ref, kmsg_ref,
):
    total = jnp.zeros((2, ROWS), F32)
    for h in range(HEADS):
        total = total + jnp.sqrt(jnp.sqrt(jnp.maximum(sums_ref[h].astype(F32), 1e-36)))
    rate = lax.rsqrt(total / (HEADS * WIDTH) + EPSILON)
    rate_ref[...] = rate
    for i in range(PIECES):
        rows = pl.ds(i * WIDTH, WIDTH)
        later = pl.ds(ROWS + i * WIDTH, WIDTH)
        span = slice(i * WIDTH, (i + 1) * WIDTH)
        q = q_ref[rows, :].astype(F32) * column(rate[0:1, span]) * qscale_ref[...]
        k = k_ref[rows, :].astype(F32) * column(rate[1:2, span]) * kscale_ref[...]
        q = q.astype(BF16)
        for x in range(SIDE):
            qmsg_ref[x, rows, :] = q
            qmsg_ref[x, later, :] = g_ref[rows, :]
        kmsg_ref[rows, :] = k.astype(BF16)
        kmsg_ref[later, :] = v_ref[rows, :]
    for x in range(SIDE):
        qmsg_ref[x, 2 * ROWS :, :] = lines_ref[...]
    kmsg_ref[2 * ROWS :, :] = lines_ref[...]


def across(lines, first):
    return jnp.concatenate([lines[first + p : first + p + 1, :] for p in range(PIECES)], axis=1)


def query_groups(qall_ref):
    rows = [qall_ref[i, 2 * ROWS :, :].astype(F32)[2 * PIECES : 2 * PIECES + 1, :] for i in range(SIDE)]
    return jnp.concatenate([row for row in rows for _ in range(PIECES)], axis=1)


def key_group(kall_ref, j):
    row = kall_ref[j, 2 * ROWS :, :].astype(F32)[2 * PIECES : 2 * PIECES + 1, :]
    return jnp.concatenate([row] * (SIDE * PIECES), axis=1)


def totals_kernel(qall_ref, kall_ref, total_ref, q_all):
    for i in range(SIDE):
        q_all[i * ROWS : (i + 1) * ROWS, :] = qall_ref[i, :ROWS, :]
    groups = query_groups(qall_ref)

    def key_block(j, total):
        scores = dot(kall_ref[j, :ROWS, :], q_all[...], NT)
        part = jnp.sum(jnp.exp2(scores * (ROOT * LOG2E)), axis=0, keepdims=True)
        return total + jnp.where(key_group(kall_ref, j) <= groups, part, 0.0)

    total = lax.fori_loop(0, SIDE, key_block, jnp.zeros((1, SIDE * ROWS), F32))
    for i in range(SIDE):
        total_ref[i] = total[:, i * ROWS : (i + 1) * ROWS]


def grads_kernel(
    place_ref, total_ref, qall_ref, kall_ref,
    inner_ref, dkv_ref, dq0_ref, dq1_ref, dq2_ref, dq3_ref,
    q_all, g_all, k_all, v_all, logs, deltas, groups, dq_acc,
):
    for i in range(SIDE):
        span = slice(i * ROWS, (i + 1) * ROWS)
        q_all[span, :] = qall_ref[i, :ROWS, :]
        g_all[span, :] = qall_ref[i, ROWS : 2 * ROWS, :]
        k_all[span, :] = kall_ref[i, :ROWS, :]
        v_all[span, :] = kall_ref[i, ROWS : 2 * ROWS, :]
        lines = qall_ref[i, 2 * ROWS :, :].astype(F32)
        deltas[:, span] = across(lines, 0) + across(lines, PIECES)
        logs[:, span] = jnp.log2(total_ref[i])
    groups[...] = query_groups(qall_ref)
    dq_acc[...] = jnp.zeros_like(dq_acc)
    inner_ref[...] = jnp.zeros_like(inner_ref)
    half = SIDE * ROWS // 2

    def key_pair(m, carry):
        rows = pl.ds(pl.multiple_of(m * half, half), half)
        keys = k_all[rows, :]
        vals = v_all[rows, :]
        shifts = [
            jnp.where(key_group(kall_ref, 2 * m + n) <= groups[...], logs[...], 1e30) for n in range(2)
        ]

        def part(h):
            span = slice(h * half, (h + 1) * half)
            queries = q_all[span, :]
            grad = g_all[span, :]
            scores = dot(keys, queries, NT)
            scaled = scores * (ROOT * LOG2E)
            upper = scaled[:ROWS] - shifts[0][:, span]
            lower = scaled[ROWS:] - shifts[1][:, span]
            probs = jnp.exp2(jnp.concatenate([upper, lower], axis=0))
            dprobs = dot(vals, grad, NT)
            dscores = probs * (dprobs - deltas[:, span])
            inner_ref[:, span] += jnp.sum(dscores * scores, axis=0, keepdims=True)
            dscores = dscores.astype(BF16)
            dq_acc[:, span] += dot(keys, dscores, TN)
            return dot(dscores, queries), dot(probs.astype(BF16), grad)

        first, second = part(0), part(1)
        dk = ((first[0] + second[0]) * ROOT).astype(BF16)
        dv = (first[1] + second[1]).astype(BF16)
        for n in range(2):
            dkv_ref[2 * m + n, :ROWS, :] = dk[n * ROWS : (n + 1) * ROWS]
            dkv_ref[2 * m + n, ROWS:, :] = dv[n * ROWS : (n + 1) * ROWS]
        return carry

    lax.fori_loop(0, SIDE // 2, key_pair, 0)
    inner_ref[...] = inner_ref[...] * ROOT
    x = place_ref[1]
    for d, ref in enumerate((dq0_ref, dq1_ref, dq2_ref, dq3_ref)):
        span = pl.ds(pl.multiple_of((x ^ d) * ROWS, ROWS), ROWS)
        ref[...] = (dq_acc[:, span].T * ROOT).astype(BF16)


def sums_kernel(
    place_ref, inner_ref, dkv_ref, dq1_ref, dq2_ref, dq3_ref, k_ref, kscale_ref,
    gk_ref, dv_ref, msg_ref, out1_ref, out2_ref, out3_ref,
):
    k_lines = []
    for i in range(PIECES):
        rows = pl.ds(i * WIDTH, WIDTH)
        later = pl.ds(ROWS + i * WIDTH, WIDTH)
        gk = sum(dkv_ref[j, rows, :].astype(F32) for j in range(SIDE)) * kscale_ref[...]
        gk_ref[rows, :] = gk
        dv_ref[rows, :] = sum(dkv_ref[j, later, :].astype(F32) for j in range(SIDE)).astype(BF16)
        k_lines.append(row_sums(gk * k_ref[rows, :].astype(F32)))
    q_line = jnp.zeros((1, ROWS), F32)
    for i in range(SIDE):
        q_line = jnp.where(place_ref[1] == i, inner_ref[:, i * ROWS : (i + 1) * ROWS], q_line)
    coded = jnp.concatenate([q_line, jnp.concatenate(k_lines, axis=1)], axis=0).astype(BF16)
    for h in range(HEADS):
        msg_ref[h] = coded
    for source, target in ((dq1_ref, out1_ref), (dq2_ref, out2_ref), (dq3_ref, out3_ref)):
        target[...] = source[...]


def final_kernel(
    sums_ref, rate_ref, dq0_ref, dq1_ref, dq2_ref, dq3_ref, gk_ref, q_ref, k_ref, qscale_ref,
    dq_ref, dk_ref,
):
    inner = jnp.zeros((2, ROWS), F32)
    for h in range(HEADS):
        inner = inner + sums_ref[h].astype(F32)
    rate = rate_ref[...]
    weight = rate * rate * inner / (HEADS * WIDTH)
    q_weight = weight[0:1, :]
    k_weight = weight[1:2, :] * rate[1:2, :]
    for i in range(PIECES):
        rows = pl.ds(i * WIDTH, WIDTH)
        span = slice(i * WIDTH, (i + 1) * WIDTH)
        gq = sum(part[rows, :].astype(F32) for part in (dq0_ref, dq1_ref, dq2_ref, dq3_ref))
        gq = gq * qscale_ref[...]
        gk = gk_ref[rows, :]
        q = q_ref[rows, :].astype(F32)
        k = k_ref[rows, :].astype(F32)
        dq_ref[rows, :] = (column(rate[0:1, span]) * gq - q * column(q_weight[:, span])).astype(BF16)
        dk_ref[rows, :] = (column(rate[1:2, span]) * gk - k * column(k_weight[:, span])).astype(BF16)


def local(q_raw, k_raw, values, out, d_out, q_gain, k_gain, order):
    block = struct((ROWS, WIDTH), BF16)
    wide = struct((ROWS, WIDTH), F32)
    pair = struct((2 * ROWS, WIDTH), BF16)
    message = struct((HEADS, 2, ROWS), BF16)
    place = jnp.stack([lax.axis_index("y"), lax.axis_index("x")]).astype(jnp.int32)
    q_gain = q_gain.reshape(1, WIDTH)
    k_gain = k_gain.reshape(1, WIDTH)

    squares = call(squares_kernel, message, limit=60)(q_raw, k_raw)
    squares = lax.all_to_all(squares, HEAD, 0, 0)
    gain = struct((1, WIDTH), F32)
    q_raw, k_raw, d_out, values, lines, q_gain, k_gain = call(
        ready_kernel,
        (block, block, block, block, struct((LINES, WIDTH), BF16), gain, gain),
        spaces="ss",
    )(place, order, q_raw, k_raw, d_out, values, out, q_gain, k_gain)
    rate, queries, keys = call(
        norms_kernel,
        (
            struct((2, ROWS), F32),
            struct((SIDE, 2 * ROWS + LINES, WIDTH), BF16),
            struct((2 * ROWS + LINES, WIDTH), BF16),
        ),
    )(squares, q_raw, k_raw, d_out, values, lines, q_gain, k_gain)
    queries = lax.all_to_all(queries, "x", 0, 0)
    keys = lax.all_gather(keys, "y", axis=0, tiled=True).reshape(SIDE, 2 * ROWS + LINES, WIDTH)

    totals = call(
        totals_kernel,
        struct((SIDE, 1, ROWS), F32),
        scratch=(pltpu.VMEM((SIDE * ROWS, WIDTH), BF16),),
    )(queries, keys)
    totals = lax.psum(totals, "x")

    tall = pltpu.VMEM((SIDE * ROWS, WIDTH), BF16)
    row = pltpu.VMEM((1, SIDE * ROWS), F32)
    inner, keys, *queries = call(
        grads_kernel,
        (
            struct((1, SIDE * ROWS), F32),
            struct((SIDE, 2 * ROWS, WIDTH), BF16),
            block, block, block, block,
        ),
        scratch=(tall, tall, tall, tall, row, row, row, pltpu.VMEM((WIDTH, SIDE * ROWS), F32)),
        spaces="s",
    )(place, totals, queries, keys)
    keys = lax.all_to_all(keys, "y", 0, 0)
    inner = lax.psum(inner, "x")
    gk, dv, inner, *queries[1:] = call(
        sums_kernel, (wide, block, message, block, block, block), spaces="s"
    )(place, inner, keys, *queries[1:], k_raw, k_gain)
    inner = lax.all_to_all(inner, HEAD, 0, 0)
    queries[1:] = [swap(part, "x", d) for d, part in enumerate(queries[1:], 1)]
    d_q, d_k = call(final_kernel, (block, block))(
        inner, rate, *queries, gk, q_raw, k_raw, q_gain
    )
    return d_q, d_k, dv


def solution(mesh):
    fine = Mesh(mesh.devices.reshape(SIDE, SIDE, 16, 2), ("y", "x", "z", "c"))
    both = P(SEQ, HEAD)
    return jax.shard_map(
        local,
        mesh=fine,
        in_specs=(both,) * 5 + (P(HEAD), P(HEAD), P()),
        out_specs=(both,) * 3,
        check_vma=False,
    )
```

```python
import math

import jax
import jax.numpy as jnp
from jax import lax
from jax.experimental import pallas as pl
from jax.experimental.pallas import tpu as pltpu
from jax.sharding import Mesh, PartitionSpec as P

EPSILON = 1e-06
SIDE = 4
HEADS = 32
ROWS = 384
WIDTH = 128
PIECES = ROWS // WIDTH
LINES = 16
HEAD = ("z", "c")
SEQ = ("y", "x")
F32 = jnp.float32
BF16 = jnp.bfloat16
ROOT = WIDTH ** (-0.5)
LOG2E = math.log2(math.e)
NT = (((1,), (1,)), ((), ()))
TN = (((0,), (0,)), ((), ()))


def swap(value, axis, mask):
    return lax.ppermute(value, axis, [(i, i ^ mask) for i in range(SIDE)])


def struct(shape, dtype):
    return jax.ShapeDtypeStruct(shape, dtype)


def call(kernel, out_shape, scratch=(), spaces="", out_spaces="", limit=32):
    def run(*args):
        memory = {"s": pltpu.SMEM, "v": pltpu.VMEM, "h": pltpu.HBM}
        leaves, tree = jax.tree.flatten(out_shape)
        out_specs = [
            pl.BlockSpec(memory_space=memory[s]) for s in out_spaces.ljust(len(leaves), "v")
        ]
        specs = [pl.BlockSpec(memory_space=memory[s]) for s in spaces.ljust(len(args), "v")]
        return pl.pallas_call(
            kernel,
            out_shape=out_shape,
            in_specs=specs,
            out_specs=jax.tree.unflatten(tree, out_specs),
            scratch_shapes=scratch,
            compiler_params=pltpu.CompilerParams(vmem_limit_bytes=limit * 2**20),
        )(*args)

    return run


def column(row):
    return jnp.broadcast_to(row, (WIDTH, WIDTH)).T


def row_sums(block):
    return jnp.sum(block.T, axis=0, keepdims=True)


def dot(a, b, dims=(((1,), (0,)), ((), ()))):
    return lax.dot_general(a, b, dims, preferred_element_type=F32)


def squares_kernel(q_ref, k_ref, msg_ref):
    sums = []
    for ref in (q_ref, k_ref):
        parts = []
        for i in range(PIECES):
            block = ref[pl.ds(i * WIDTH, WIDTH), :].astype(F32)
            parts.append(row_sums(block * block))
        sums.append(jnp.concatenate(parts, axis=1))
    both = jnp.concatenate(sums, axis=0)
    square = both * both
    coded = (square * square).astype(BF16)
    for h in range(HEADS):
        msg_ref[h] = coded


def ready_kernel(
    place_ref, order_ref, g_ref, o_ref, v_ref, qgain_ref, kgain_ref,
    g_out, v_out, lines_ref, qscale_ref, kscale_ref,
):
    group = order_ref[place_ref[0] * SIDE + place_ref[1]].astype(F32)
    line = lax.broadcasted_iota(jnp.int32, (LINES, WIDTH), 0)
    lines = jnp.full((LINES, WIDTH), group, F32)
    for i in range(PIECES):
        rows = pl.ds(i * WIDTH, WIDTH)
        delta = row_sums(o_ref[rows, :].astype(F32) * g_ref[rows, :].astype(F32))
        high = delta.astype(BF16).astype(F32)
        lines = jnp.where(line == i, high, lines)
        lines = jnp.where(line == PIECES + i, delta - high, lines)
    lines_ref[...] = lines.astype(BF16)
    g_out[...] = g_ref[...]
    v_out[...] = v_ref[...]
    qscale_ref[...] = qgain_ref[...].astype(F32)
    kscale_ref[...] = kgain_ref[...].astype(F32)


def norms_kernel(
    sums_ref, q_ref, k_ref, g_ref, v_ref, lines_ref, qscale_ref, kscale_ref,
    rate_ref, qmsg_hbm, kmsg_ref, q_buf, sems,
):
    early = pl.ds(ROWS, ROWS + LINES)
    late = pl.ds(0, ROWS)
    copies = [
        [
            pltpu.make_async_copy(q_buf.at[rows, :], qmsg_hbm.at[x, rows, :], sems.at[n, x])
            for x in range(SIDE)
        ]
        for n, rows in enumerate((early, late))
    ]
    q_buf[ROWS : 2 * ROWS, :] = g_ref[...]
    q_buf[2 * ROWS :, :] = lines_ref[...]
    for copy in copies[0]:
        copy.start()
    total = jnp.zeros((2, ROWS), F32)
    for h in range(HEADS):
        total = total + lax.rsqrt(lax.rsqrt(jnp.maximum(sums_ref[h].astype(F32), 1e-36)))
    rate = lax.rsqrt(total / (HEADS * WIDTH) + EPSILON)
    rate_ref[...] = rate
    for i in range(PIECES):
        rows = pl.ds(i * WIDTH, WIDTH)
        span = slice(i * WIDTH, (i + 1) * WIDTH)
        q = q_ref[rows, :].astype(F32) * column(rate[0:1, span]) * qscale_ref[...]
        q_buf[rows, :] = q.astype(BF16)
    for copy in copies[1]:
        copy.start()
    for i in range(PIECES):
        rows = pl.ds(i * WIDTH, WIDTH)
        span = slice(i * WIDTH, (i + 1) * WIDTH)
        k = k_ref[rows, :].astype(F32) * column(rate[1:2, span]) * kscale_ref[...]
        kmsg_ref[rows, :] = k.astype(BF16)
    kmsg_ref[ROWS : 2 * ROWS, :] = v_ref[...]
    kmsg_ref[2 * ROWS :, :] = lines_ref[...]
    for copy in copies[0] + copies[1]:
        copy.wait()


def across(lines, first):
    return jnp.concatenate([lines[first + p : first + p + 1, :] for p in range(PIECES)], axis=1)


def query_groups(qall_ref):
    rows = [qall_ref[i, 2 * ROWS :, :].astype(F32)[2 * PIECES : 2 * PIECES + 1, :] for i in range(SIDE)]
    return jnp.concatenate([row for row in rows for _ in range(PIECES)], axis=1)


def key_group(kall_ref, j):
    row = kall_ref[j, 2 * ROWS :, :].astype(F32)[2 * PIECES : 2 * PIECES + 1, :]
    return jnp.concatenate([row] * (SIDE * PIECES), axis=1)


def totals_kernel(qall_ref, kall_ref, total_ref, q_all):
    for i in range(SIDE):
        q_all[i * ROWS : (i + 1) * ROWS, :] = qall_ref[i, :ROWS, :]
    groups = query_groups(qall_ref)

    def key_block(j, total):
        scores = dot(kall_ref[j, :ROWS, :], q_all[...], NT)
        part = jnp.sum(jnp.exp2(scores * (ROOT * LOG2E)), axis=0, keepdims=True)
        return total + jnp.where(key_group(kall_ref, j) <= groups, part, 0.0)

    total = lax.fori_loop(0, SIDE, key_block, jnp.zeros((1, SIDE * ROWS), F32))
    for i in range(SIDE):
        total_ref[i] = total[:, i * ROWS : (i + 1) * ROWS]


def grads_kernel(
    total_ref, qall_ref, kall_ref,
    inner_ref, dkv_hbm, dq_ref,
    q_all, g_all, k_all, v_all, logs, deltas, groups, dq_acc, dkv_buf, sems,
):
    for i in range(SIDE):
        span = slice(i * ROWS, (i + 1) * ROWS)
        q_all[span, :] = qall_ref[i, :ROWS, :]
        g_all[span, :] = qall_ref[i, ROWS : 2 * ROWS, :]
        k_all[span, :] = kall_ref[i, :ROWS, :]
        v_all[span, :] = kall_ref[i, ROWS : 2 * ROWS, :]
        lines = qall_ref[i, 2 * ROWS :, :].astype(F32)
        deltas[:, span] = across(lines, 0) + across(lines, PIECES)
        logs[:, span] = jnp.log2(total_ref[i])
    groups[...] = query_groups(qall_ref)
    dq_acc[...] = jnp.zeros_like(dq_acc)
    half = SIDE * ROWS // 2

    def leave(m):
        pair = pl.ds(2 * m, 2)
        return pltpu.make_async_copy(dkv_buf.at[pair], dkv_hbm.at[pair], sems.at[m])

    def key_pair(m, carry):
        rows = pl.ds(pl.multiple_of(m * half, half), half)
        keys = k_all[rows, :]
        vals = v_all[rows, :]
        shifts = [
            jnp.where(key_group(kall_ref, 2 * m + n) <= groups[...], logs[...], 1e30) for n in range(2)
        ]

        def part(h):
            span = slice(h * half, (h + 1) * half)
            queries = q_all[span, :]
            grad = g_all[span, :]
            scores = dot(keys, queries, NT) * (ROOT * LOG2E)
            upper = scores[:ROWS] - shifts[0][:, span]
            lower = scores[ROWS:] - shifts[1][:, span]
            probs = jnp.exp2(jnp.concatenate([upper, lower], axis=0))
            dprobs = dot(vals, grad, NT)
            dscores = (probs * (dprobs - deltas[:, span])).astype(BF16)
            dq_acc[:, span] += dot(keys, dscores, TN)
            return dot(dscores, queries), dot(probs.astype(BF16), grad)

        first, second = part(0), part(1)
        dk = ((first[0] + second[0]) * ROOT).astype(BF16)
        dv = (first[1] + second[1]).astype(BF16)
        for n in range(2):
            dkv_buf[2 * m + n, :ROWS, :] = dk[n * ROWS : (n + 1) * ROWS]
            dkv_buf[2 * m + n, ROWS:, :] = dv[n * ROWS : (n + 1) * ROWS]
        leave(m).start()
        return carry

    lax.fori_loop(0, SIDE // 2, key_pair, 0)
    for p in range(SIDE * PIECES):
        span = slice(p * WIDTH, (p + 1) * WIDTH)
        product = dq_acc[:, span] * q_all[span, :].astype(F32).T
        inner_ref[:, span] = jnp.sum(product, axis=0, keepdims=True) * ROOT
    for i in range(SIDE):
        dq_ref[i] = (dq_acc[:, i * ROWS : (i + 1) * ROWS].T * ROOT).astype(BF16)
    for m in range(SIDE // 2):
        leave(m).wait()


def sums_kernel(
    place_ref, inner_ref, dkv_ref, dq_ref, k_ref, kscale_ref,
    gk_ref, msg_ref, out0_ref, out1_ref, out2_ref, out3_ref,
):
    k_lines = []
    for i in range(PIECES):
        rows = pl.ds(i * WIDTH, WIDTH)
        gk = sum(dkv_ref[j, rows, :].astype(F32) for j in range(SIDE)) * kscale_ref[...]
        gk_ref[rows, :] = gk
        k_lines.append(row_sums(gk * k_ref[rows, :].astype(F32)))
    q_line = jnp.zeros((1, ROWS), F32)
    for i in range(SIDE):
        q_line = jnp.where(place_ref[1] == i, inner_ref[:, i * ROWS : (i + 1) * ROWS], q_line)
    coded = jnp.concatenate([q_line, jnp.concatenate(k_lines, axis=1)], axis=0).astype(BF16)
    for h in range(HEADS):
        msg_ref[h] = coded
    for d, target in enumerate((out0_ref, out1_ref, out2_ref, out3_ref)):
        target[...] = dq_ref[place_ref[1] ^ d]


def values_kernel(dkv_ref, dv_ref):
    dv_ref[...] = sum(dkv_ref[j, ROWS:, :].astype(F32) for j in range(SIDE)).astype(BF16)


def final_kernel(
    sums_ref, rate_ref, dq0_ref, dq1_ref, dq2_ref, dq3_ref, gk_ref, q_ref, k_ref, qscale_ref,
    dq_ref, dk_ref,
):
    inner = jnp.zeros((2, ROWS), F32)
    for h in range(HEADS):
        inner = inner + sums_ref[h].astype(F32)
    rate = rate_ref[...]
    weight = rate * rate * inner / (HEADS * WIDTH)
    q_weight = weight[0:1, :]
    k_weight = weight[1:2, :] * rate[1:2, :]
    for i in range(PIECES):
        rows = pl.ds(i * WIDTH, WIDTH)
        span = slice(i * WIDTH, (i + 1) * WIDTH)
        gq = sum(part[rows, :].astype(F32) for part in (dq0_ref, dq1_ref, dq2_ref, dq3_ref))
        gq = gq * qscale_ref[...]
        gk = gk_ref[rows, :]
        q = q_ref[rows, :].astype(F32)
        k = k_ref[rows, :].astype(F32)
        dq_ref[rows, :] = (column(rate[0:1, span]) * gq - q * column(q_weight[:, span])).astype(BF16)
        dk_ref[rows, :] = (column(rate[1:2, span]) * gk - k * column(k_weight[:, span])).astype(BF16)


def local(q_raw, k_raw, values, out, d_out, q_gain, k_gain, order):
    block = struct((ROWS, WIDTH), BF16)
    wide = struct((ROWS, WIDTH), F32)
    pair = struct((2 * ROWS, WIDTH), BF16)
    message = struct((HEADS, 2, ROWS), BF16)
    place = jnp.stack([lax.axis_index("y"), lax.axis_index("x")]).astype(jnp.int32)
    q_gain = q_gain.reshape(1, WIDTH)
    k_gain = k_gain.reshape(1, WIDTH)

    squares = call(squares_kernel, message, limit=60)(q_raw, k_raw)
    squares = lax.all_to_all(squares, HEAD, 0, 0)
    gain = struct((1, WIDTH), F32)
    d_out, values, lines, q_gain, k_gain = call(
        ready_kernel,
        (block, block, struct((LINES, WIDTH), BF16), gain, gain),
        spaces="ss",
    )(place, order, d_out, out, values, q_gain, k_gain)
    rate, queries, keys = call(
        norms_kernel,
        (
            struct((2, ROWS), F32),
            struct((SIDE, 2 * ROWS + LINES, WIDTH), BF16),
            struct((2 * ROWS + LINES, WIDTH), BF16),
        ),
        scratch=(
            pltpu.VMEM((2 * ROWS + LINES, WIDTH), BF16),
            pltpu.SemaphoreType.DMA((2, SIDE)),
        ),
        out_spaces="vh",
    )(squares, q_raw, k_raw, d_out, values, lines, q_gain, k_gain)
    queries = lax.all_to_all(queries, "x", 0, 0)
    keys = lax.all_gather(keys, "y", axis=0, tiled=True).reshape(SIDE, 2 * ROWS + LINES, WIDTH)

    totals = call(
        totals_kernel,
        struct((SIDE, 1, ROWS), F32),
        scratch=(pltpu.VMEM((SIDE * ROWS, WIDTH), BF16),),
    )(queries, keys)
    totals = lax.psum(totals, "x")

    tall = pltpu.VMEM((SIDE * ROWS, WIDTH), BF16)
    row = pltpu.VMEM((1, SIDE * ROWS), F32)
    inner, keys, queries = call(
        grads_kernel,
        (
            struct((1, SIDE * ROWS), F32),
            struct((SIDE, 2 * ROWS, WIDTH), BF16),
            struct((SIDE, ROWS, WIDTH), BF16),
        ),
        scratch=(
            tall, tall, tall, tall, row, row, row,
            pltpu.VMEM((WIDTH, SIDE * ROWS), F32),
            pltpu.VMEM((SIDE, 2 * ROWS, WIDTH), BF16),
            pltpu.SemaphoreType.DMA((SIDE // 2,)),
        ),
        out_spaces="vh",
    )(totals, queries, keys)
    keys = lax.all_to_all(keys, "y", 0, 0)
    inner = lax.psum(inner, "x")
    dv = call(values_kernel, block)(keys)
    gk, inner, *queries = call(
        sums_kernel, (wide, message, block, block, block, block), spaces="s"
    )(place, inner, keys, queries, k_raw, k_gain)
    inner = lax.all_to_all(inner, HEAD, 0, 0)
    queries[1:] = [swap(part, "x", d) for d, part in enumerate(queries[1:], 1)]
    d_q, d_k = call(final_kernel, (block, block))(
        inner, rate, *queries, gk, q_raw, k_raw, q_gain
    )
    return d_q, d_k, dv


def solution(mesh):
    fine = Mesh(mesh.devices.reshape(SIDE, SIDE, 16, 2), ("y", "x", "z", "c"))
    both = P(SEQ, HEAD)
    return jax.shard_map(
        local,
        mesh=fine,
        in_specs=(both,) * 5 + (P(HEAD), P(HEAD), P()),
        out_specs=(both,) * 3,
        check_vma=False,
    )
```

```python
import math

import jax
import jax.numpy as jnp
from jax import lax
from jax.experimental import pallas as pl
from jax.experimental.pallas import tpu as pltpu
from jax.sharding import Mesh, PartitionSpec as P

EPSILON = 1e-06
SIDE = 4
HEADS = 32
ROWS = 384
WIDTH = 128
PIECES = ROWS // WIDTH
LINES = 16
HEAD = ("z", "c")
SEQ = ("y", "x")
F32 = jnp.float32
BF16 = jnp.bfloat16
ROOT = WIDTH ** (-0.5)
LOG2E = math.log2(math.e)
NT = (((1,), (1,)), ((), ()))
TN = (((0,), (0,)), ((), ()))


def swap(value, axis, mask):
    return lax.ppermute(value, axis, [(i, i ^ mask) for i in range(SIDE)])


def struct(shape, dtype):
    return jax.ShapeDtypeStruct(shape, dtype)


def call(kernel, out_shape, scratch=(), spaces="", out_spaces="", limit=32):
    def run(*args):
        memory = {"s": pltpu.SMEM, "v": pltpu.VMEM, "h": pltpu.HBM}
        leaves, tree = jax.tree.flatten(out_shape)
        out_specs = [
            pl.BlockSpec(memory_space=memory[s]) for s in out_spaces.ljust(len(leaves), "v")
        ]
        specs = [pl.BlockSpec(memory_space=memory[s]) for s in spaces.ljust(len(args), "v")]
        return pl.pallas_call(
            kernel,
            out_shape=out_shape,
            in_specs=specs,
            out_specs=jax.tree.unflatten(tree, out_specs),
            scratch_shapes=scratch,
            compiler_params=pltpu.CompilerParams(vmem_limit_bytes=limit * 2**20),
        )(*args)

    return run


def column(row):
    return jnp.broadcast_to(row, (WIDTH, WIDTH)).T


def row_sums(block):
    return jnp.sum(block.T, axis=0, keepdims=True)


def dot(a, b, dims=(((1,), (0,)), ((), ()))):
    return lax.dot_general(a, b, dims, preferred_element_type=F32)


def encode(value):
    square = value * value
    return (square * square).astype(BF16)


def decode(coded):
    return lax.rsqrt(lax.rsqrt(jnp.maximum(coded.astype(F32), 1e-36)))


def squares_kernel(q_ref, k_ref, msg_ref, own_ref):
    sums = []
    for ref in (q_ref, k_ref):
        parts = []
        for i in range(PIECES):
            block = ref[pl.ds(i * WIDTH, WIDTH), :].astype(F32)
            parts.append(row_sums(block * block))
        sums.append(jnp.concatenate(parts, axis=1))
    both = jnp.concatenate(sums, axis=0)
    own_ref[...] = both
    coded = encode(both)
    for h in range(HEADS):
        msg_ref[h] = coded


def ready_kernel(
    place_ref, order_ref, own_ref, g_ref, o_ref, v_ref, qgain_ref, kgain_ref,
    own_out, g_out, v_out, lines_ref, qscale_ref, kscale_ref,
):
    group = order_ref[place_ref[0] * SIDE + place_ref[1]].astype(F32)
    line = lax.broadcasted_iota(jnp.int32, (LINES, WIDTH), 0)
    lines = jnp.full((LINES, WIDTH), group, F32)
    for i in range(PIECES):
        rows = pl.ds(i * WIDTH, WIDTH)
        delta = row_sums(o_ref[rows, :].astype(F32) * g_ref[rows, :].astype(F32))
        high = delta.astype(BF16).astype(F32)
        lines = jnp.where(line == i, high, lines)
        lines = jnp.where(line == PIECES + i, delta - high, lines)
    lines_ref[...] = lines.astype(BF16)
    own_out[...] = own_ref[...]
    g_out[...] = g_ref[...]
    v_out[...] = v_ref[...]
    qscale_ref[...] = qgain_ref[...].astype(F32)
    kscale_ref[...] = kgain_ref[...].astype(F32)


def norms_kernel(
    sums_ref, own_ref, q_ref, k_ref, g_ref, v_ref, lines_ref, qscale_ref, kscale_ref,
    rate_ref, qmsg_hbm, kmsg_ref, q_buf, sems,
):
    early = pl.ds(ROWS, ROWS + LINES)
    late = pl.ds(0, ROWS)
    copies = [
        [
            pltpu.make_async_copy(q_buf.at[rows, :], qmsg_hbm.at[x, rows, :], sems.at[n, x])
            for x in range(SIDE)
        ]
        for n, rows in enumerate((early, late))
    ]
    q_buf[ROWS : 2 * ROWS, :] = g_ref[...]
    q_buf[2 * ROWS :, :] = lines_ref[...]
    for copy in copies[0]:
        copy.start()
    total = own_ref[...] - decode(encode(own_ref[...]))
    for h in range(HEADS):
        total = total + decode(sums_ref[h])
    total = jnp.maximum(total, own_ref[...])
    rate = lax.rsqrt(total / (HEADS * WIDTH) + EPSILON)
    rate_ref[...] = rate
    for i in range(PIECES):
        rows = pl.ds(i * WIDTH, WIDTH)
        span = slice(i * WIDTH, (i + 1) * WIDTH)
        q = q_ref[rows, :].astype(F32) * column(rate[0:1, span]) * qscale_ref[...]
        q_buf[rows, :] = q.astype(BF16)
    for copy in copies[1]:
        copy.start()
    for i in range(PIECES):
        rows = pl.ds(i * WIDTH, WIDTH)
        span = slice(i * WIDTH, (i + 1) * WIDTH)
        k = k_ref[rows, :].astype(F32) * column(rate[1:2, span]) * kscale_ref[...]
        kmsg_ref[rows, :] = k.astype(BF16)
    kmsg_ref[ROWS : 2 * ROWS, :] = v_ref[...]
    kmsg_ref[2 * ROWS :, :] = lines_ref[...]
    for copy in copies[0] + copies[1]:
        copy.wait()


def across(lines, first):
    return jnp.concatenate([lines[first + p : first + p + 1, :] for p in range(PIECES)], axis=1)


def query_groups(qall_ref):
    rows = [qall_ref[i, 2 * ROWS :, :].astype(F32)[2 * PIECES : 2 * PIECES + 1, :] for i in range(SIDE)]
    return jnp.concatenate([row for row in rows for _ in range(PIECES)], axis=1)


def key_group(kall_ref, j):
    row = kall_ref[j, 2 * ROWS :, :].astype(F32)[2 * PIECES : 2 * PIECES + 1, :]
    return jnp.concatenate([row] * (SIDE * PIECES), axis=1)


def totals_kernel(qall_ref, kall_ref, total_ref, q_all):
    for i in range(SIDE):
        q_all[i * ROWS : (i + 1) * ROWS, :] = qall_ref[i, :ROWS, :]
    groups = query_groups(qall_ref)

    def key_block(j, total):
        scores = dot(kall_ref[j, :ROWS, :], q_all[...], NT)
        part = jnp.sum(jnp.exp2(scores * (ROOT * LOG2E)), axis=0, keepdims=True)
        return total + jnp.where(key_group(kall_ref, j) <= groups, part, 0.0)

    total = lax.fori_loop(0, SIDE, key_block, jnp.zeros((1, SIDE * ROWS), F32))
    for i in range(SIDE):
        total_ref[i] = total[:, i * ROWS : (i + 1) * ROWS]


def grads_kernel(
    total_ref, qall_ref, kall_ref,
    inner_ref, dkv_hbm, dq_ref,
    q_all, g_all, k_all, v_all, logs, deltas, groups, dq_acc, dkv_buf, sems,
):
    for i in range(SIDE):
        span = slice(i * ROWS, (i + 1) * ROWS)
        q_all[span, :] = qall_ref[i, :ROWS, :]
        g_all[span, :] = qall_ref[i, ROWS : 2 * ROWS, :]
        k_all[span, :] = kall_ref[i, :ROWS, :]
        v_all[span, :] = kall_ref[i, ROWS : 2 * ROWS, :]
        lines = qall_ref[i, 2 * ROWS :, :].astype(F32)
        deltas[:, span] = across(lines, 0) + across(lines, PIECES)
        logs[:, span] = jnp.log2(total_ref[i])
    groups[...] = query_groups(qall_ref)
    dq_acc[...] = jnp.zeros_like(dq_acc)
    half = SIDE * ROWS // 2

    def leave(m):
        pair = pl.ds(2 * m, 2)
        return pltpu.make_async_copy(dkv_buf.at[pair], dkv_hbm.at[pair], sems.at[m])

    def key_pair(m, carry):
        rows = pl.ds(pl.multiple_of(m * half, half), half)
        keys = k_all[rows, :]
        vals = v_all[rows, :]
        shifts = [
            jnp.where(key_group(kall_ref, 2 * m + n) <= groups[...], logs[...], 1e30) for n in range(2)
        ]

        def part(h):
            span = slice(h * half, (h + 1) * half)
            queries = q_all[span, :]
            grad = g_all[span, :]
            scores = dot(keys, queries, NT) * (ROOT * LOG2E)
            upper = scores[:ROWS] - shifts[0][:, span]
            lower = scores[ROWS:] - shifts[1][:, span]
            probs = jnp.exp2(jnp.concatenate([upper, lower], axis=0))
            dprobs = dot(vals, grad, NT)
            dscores = (probs * (dprobs - deltas[:, span])).astype(BF16)
            dq_acc[:, span] += dot(keys, dscores, TN)
            return dot(dscores, queries), dot(probs.astype(BF16), grad)

        first, second = part(0), part(1)
        dk = ((first[0] + second[0]) * ROOT).astype(BF16)
        dv = (first[1] + second[1]).astype(BF16)
        for n in range(2):
            dkv_buf[2 * m + n, :ROWS, :] = dk[n * ROWS : (n + 1) * ROWS]
            dkv_buf[2 * m + n, ROWS:, :] = dv[n * ROWS : (n + 1) * ROWS]
        leave(m).start()
        return carry

    lax.fori_loop(0, SIDE // 2, key_pair, 0)
    for p in range(SIDE * PIECES):
        span = slice(p * WIDTH, (p + 1) * WIDTH)
        product = dq_acc[:, span] * q_all[span, :].astype(F32).T
        inner_ref[:, span] = jnp.sum(product, axis=0, keepdims=True) * ROOT
    for i in range(SIDE):
        dq_ref[i] = (dq_acc[:, i * ROWS : (i + 1) * ROWS].T * ROOT).astype(BF16)
    for m in range(SIDE // 2):
        leave(m).wait()


def sums_kernel(
    place_ref, inner_ref, dkv_ref, dq_ref, k_ref, kscale_ref,
    gk_ref, msg_ref, own_ref, out0_ref, out1_ref, out2_ref, out3_ref,
):
    k_lines = []
    for i in range(PIECES):
        rows = pl.ds(i * WIDTH, WIDTH)
        gk = sum(dkv_ref[j, rows, :].astype(F32) for j in range(SIDE)) * kscale_ref[...]
        gk_ref[rows, :] = gk
        k_lines.append(row_sums(gk * k_ref[rows, :].astype(F32)))
    q_line = jnp.zeros((1, ROWS), F32)
    for i in range(SIDE):
        q_line = jnp.where(place_ref[1] == i, inner_ref[:, i * ROWS : (i + 1) * ROWS], q_line)
    both = jnp.concatenate([q_line, jnp.concatenate(k_lines, axis=1)], axis=0)
    own_ref[...] = both
    coded = both.astype(BF16)
    for h in range(HEADS):
        msg_ref[h] = coded
    for d, target in enumerate((out0_ref, out1_ref, out2_ref, out3_ref)):
        target[...] = dq_ref[place_ref[1] ^ d]


def values_kernel(dkv_ref, dv_ref):
    dv_ref[...] = sum(dkv_ref[j, ROWS:, :].astype(F32) for j in range(SIDE)).astype(BF16)


def final_kernel(
    sums_ref, own_ref, rate_ref, dq0_ref, dq1_ref, dq2_ref, dq3_ref, gk_ref, q_ref, k_ref, qscale_ref,
    dq_ref, dk_ref,
):
    inner = own_ref[...] - own_ref[...].astype(BF16).astype(F32)
    for h in range(HEADS):
        inner = inner + sums_ref[h].astype(F32)
    rate = rate_ref[...]
    weight = rate * rate * inner / (HEADS * WIDTH)
    q_weight = weight[0:1, :]
    k_weight = weight[1:2, :] * rate[1:2, :]
    for i in range(PIECES):
        rows = pl.ds(i * WIDTH, WIDTH)
        span = slice(i * WIDTH, (i + 1) * WIDTH)
        gq = sum(part[rows, :].astype(F32) for part in (dq0_ref, dq1_ref, dq2_ref, dq3_ref))
        gq = gq * qscale_ref[...]
        gk = gk_ref[rows, :]
        q = q_ref[rows, :].astype(F32)
        k = k_ref[rows, :].astype(F32)
        dq_ref[rows, :] = (column(rate[0:1, span]) * gq - q * column(q_weight[:, span])).astype(BF16)
        dk_ref[rows, :] = (column(rate[1:2, span]) * gk - k * column(k_weight[:, span])).astype(BF16)


def local(q_raw, k_raw, values, out, d_out, q_gain, k_gain, order):
    block = struct((ROWS, WIDTH), BF16)
    wide = struct((ROWS, WIDTH), F32)
    pair = struct((2 * ROWS, WIDTH), BF16)
    message = struct((HEADS, 2, ROWS), BF16)
    place = jnp.stack([lax.axis_index("y"), lax.axis_index("x")]).astype(jnp.int32)
    q_gain = q_gain.reshape(1, WIDTH)
    k_gain = k_gain.reshape(1, WIDTH)

    exact = struct((2, ROWS), F32)
    squares, own_squares = call(squares_kernel, (message, exact), limit=60)(q_raw, k_raw)
    squares = lax.all_to_all(squares, HEAD, 0, 0)
    gain = struct((1, WIDTH), F32)
    own_squares, d_out, values, lines, q_gain, k_gain = call(
        ready_kernel,
        (exact, block, block, struct((LINES, WIDTH), BF16), gain, gain),
        spaces="ss",
    )(place, order, own_squares, d_out, out, values, q_gain, k_gain)
    rate, queries, keys = call(
        norms_kernel,
        (
            struct((2, ROWS), F32),
            struct((SIDE, 2 * ROWS + LINES, WIDTH), BF16),
            struct((2 * ROWS + LINES, WIDTH), BF16),
        ),
        scratch=(
            pltpu.VMEM((2 * ROWS + LINES, WIDTH), BF16),
            pltpu.SemaphoreType.DMA((2, SIDE)),
        ),
        out_spaces="vh",
    )(squares, own_squares, q_raw, k_raw, d_out, values, lines, q_gain, k_gain)
    queries = lax.all_to_all(queries, "x", 0, 0)
    keys = lax.all_gather(keys, "y", axis=0, tiled=True).reshape(SIDE, 2 * ROWS + LINES, WIDTH)

    totals = call(
        totals_kernel,
        struct((SIDE, 1, ROWS), F32),
        scratch=(pltpu.VMEM((SIDE * ROWS, WIDTH), BF16),),
    )(queries, keys)
    totals = lax.psum(totals, "x")

    tall = pltpu.VMEM((SIDE * ROWS, WIDTH), BF16)
    row = pltpu.VMEM((1, SIDE * ROWS), F32)
    inner, keys, queries = call(
        grads_kernel,
        (
            struct((1, SIDE * ROWS), F32),
            struct((SIDE, 2 * ROWS, WIDTH), BF16),
            struct((SIDE, ROWS, WIDTH), BF16),
        ),
        scratch=(
            tall, tall, tall, tall, row, row, row,
            pltpu.VMEM((WIDTH, SIDE * ROWS), F32),
            pltpu.VMEM((SIDE, 2 * ROWS, WIDTH), BF16),
            pltpu.SemaphoreType.DMA((SIDE // 2,)),
        ),
        out_spaces="vh",
    )(totals, queries, keys)
    keys = lax.all_to_all(keys, "y", 0, 0)
    inner = lax.psum(inner, "x")
    dv = call(values_kernel, block)(keys)
    gk, inner, own_inner, *queries = call(
        sums_kernel, (wide, message, exact, block, block, block, block), spaces="s"
    )(place, inner, keys, queries, k_raw, k_gain)
    inner = lax.all_to_all(inner, HEAD, 0, 0)
    queries[1:] = [swap(part, "x", d) for d, part in enumerate(queries[1:], 1)]
    d_q, d_k = call(final_kernel, (block, block))(
        inner, own_inner, rate, *queries, gk, q_raw, k_raw, q_gain
    )
    return d_q, d_k, dv


def solution(mesh):
    fine = Mesh(mesh.devices.reshape(SIDE, SIDE, 16, 2), ("y", "x", "z", "c"))
    both = P(SEQ, HEAD)
    return jax.shard_map(
        local,
        mesh=fine,
        in_specs=(both,) * 5 + (P(HEAD), P(HEAD), P()),
        out_specs=(both,) * 3,
        check_vma=False,
    )
```

```python
import math

import jax
import jax.numpy as jnp
from jax import lax
from jax.experimental import pallas as pl
from jax.experimental.pallas import tpu as pltpu
from jax.sharding import Mesh, PartitionSpec as P

EPSILON = 1e-06
SIDE = 4
HEADS = 32
ROWS = 384
WIDTH = 128
PIECES = ROWS // WIDTH
LINES = 16
HEAD = ("z", "c")
SEQ = ("y", "x")
F32 = jnp.float32
BF16 = jnp.bfloat16
ROOT = WIDTH ** (-0.5)
LOG2E = math.log2(math.e)
NT = (((1,), (1,)), ((), ()))
TN = (((0,), (0,)), ((), ()))


def swap(value, axis, mask):
    return lax.ppermute(value, axis, [(i, i ^ mask) for i in range(SIDE)])


def struct(shape, dtype):
    return jax.ShapeDtypeStruct(shape, dtype)


def call(kernel, out_shape, scratch=(), spaces="", out_spaces="", limit=32):
    def run(*args):
        memory = {"s": pltpu.SMEM, "v": pltpu.VMEM, "h": pltpu.HBM}
        leaves, tree = jax.tree.flatten(out_shape)
        out_specs = [
            pl.BlockSpec(memory_space=memory[s]) for s in out_spaces.ljust(len(leaves), "v")
        ]
        specs = [pl.BlockSpec(memory_space=memory[s]) for s in spaces.ljust(len(args), "v")]
        return pl.pallas_call(
            kernel,
            out_shape=out_shape,
            in_specs=specs,
            out_specs=jax.tree.unflatten(tree, out_specs),
            scratch_shapes=scratch,
            compiler_params=pltpu.CompilerParams(vmem_limit_bytes=limit * 2**20),
        )(*args)

    return run


def column(row):
    return jnp.broadcast_to(row, (WIDTH, WIDTH)).T


def row_sums(block):
    return jnp.sum(block.T, axis=0, keepdims=True)


def dot(a, b, dims=(((1,), (0,)), ((), ()))):
    return lax.dot_general(a, b, dims, preferred_element_type=F32)


def encode(value):
    square = value * value
    return (square * square).astype(BF16)


def decode(coded):
    return lax.rsqrt(lax.rsqrt(jnp.maximum(coded.astype(F32), 1e-36)))


def squares_kernel(q_ref, k_ref, msg_ref, own_ref):
    sums = []
    for ref in (q_ref, k_ref):
        parts = []
        for i in range(PIECES):
            block = ref[pl.ds(i * WIDTH, WIDTH), :].astype(F32)
            parts.append(row_sums(block * block))
        sums.append(jnp.concatenate(parts, axis=1))
    both = jnp.concatenate(sums, axis=0)
    own_ref[...] = both
    coded = encode(both)
    for h in range(HEADS):
        msg_ref[h] = coded


def ready_kernel(
    place_ref, order_ref, own_ref, g_ref, o_ref, v_ref, qgain_ref, kgain_ref,
    own_out, g_out, v_out, lines_ref, qscale_ref, kscale_ref,
):
    group = order_ref[place_ref[0] * SIDE + place_ref[1]].astype(F32)
    line = lax.broadcasted_iota(jnp.int32, (LINES, WIDTH), 0)
    lines = jnp.full((LINES, WIDTH), group, F32)
    for i in range(PIECES):
        rows = pl.ds(i * WIDTH, WIDTH)
        delta = row_sums(o_ref[rows, :].astype(F32) * g_ref[rows, :].astype(F32))
        high = delta.astype(BF16).astype(F32)
        lines = jnp.where(line == i, high, lines)
        lines = jnp.where(line == PIECES + i, delta - high, lines)
    lines_ref[...] = lines.astype(BF16)
    own_out[...] = own_ref[...]
    g_out[...] = g_ref[...]
    v_out[...] = v_ref[...]
    qscale_ref[...] = qgain_ref[...].astype(F32)
    kscale_ref[...] = kgain_ref[...].astype(F32)


def norms_kernel(
    sums_ref, own_ref, q_ref, k_ref, g_ref, v_ref, lines_ref, qscale_ref, kscale_ref,
    rate_ref, qmsg_hbm, kmsg_ref, q_buf, sems,
):
    early = pl.ds(ROWS, ROWS + LINES)
    late = pl.ds(0, ROWS)
    copies = [
        [
            pltpu.make_async_copy(q_buf.at[rows, :], qmsg_hbm.at[x, rows, :], sems.at[n, x])
            for x in range(SIDE)
        ]
        for n, rows in enumerate((early, late))
    ]
    q_buf[ROWS : 2 * ROWS, :] = g_ref[...]
    q_buf[2 * ROWS :, :] = lines_ref[...]
    for copy in copies[0]:
        copy.start()
    total = own_ref[...] - decode(encode(own_ref[...]))
    for h in range(HEADS):
        total = total + decode(sums_ref[h])
    total = jnp.maximum(total, own_ref[...])
    rate = lax.rsqrt(total / (HEADS * WIDTH) + EPSILON)
    rate_ref[...] = rate
    for i in range(PIECES):
        rows = pl.ds(i * WIDTH, WIDTH)
        span = slice(i * WIDTH, (i + 1) * WIDTH)
        q = q_ref[rows, :].astype(F32) * column(rate[0:1, span]) * qscale_ref[...]
        q_buf[rows, :] = q.astype(BF16)
    for copy in copies[1]:
        copy.start()
    for i in range(PIECES):
        rows = pl.ds(i * WIDTH, WIDTH)
        span = slice(i * WIDTH, (i + 1) * WIDTH)
        k = k_ref[rows, :].astype(F32) * column(rate[1:2, span]) * kscale_ref[...]
        kmsg_ref[rows, :] = k.astype(BF16)
    kmsg_ref[ROWS : 2 * ROWS, :] = v_ref[...]
    kmsg_ref[2 * ROWS :, :] = lines_ref[...]
    for copy in copies[0] + copies[1]:
        copy.wait()


def across(lines, first):
    return jnp.concatenate([lines[first + p : first + p + 1, :] for p in range(PIECES)], axis=1)


def query_groups(qall_ref):
    rows = [qall_ref[i, 2 * ROWS :, :].astype(F32)[2 * PIECES : 2 * PIECES + 1, :] for i in range(SIDE)]
    return jnp.concatenate([row for row in rows for _ in range(PIECES)], axis=1)


def key_group(kall_ref, j):
    row = kall_ref[j, 2 * ROWS :, :].astype(F32)[2 * PIECES : 2 * PIECES + 1, :]
    return jnp.concatenate([row] * (SIDE * PIECES), axis=1)


def totals_kernel(qall_ref, kall_ref, total_ref, q_all):
    for i in range(SIDE):
        q_all[i * ROWS : (i + 1) * ROWS, :] = qall_ref[i, :ROWS, :]
    groups = query_groups(qall_ref)

    def key_block(j, total):
        scores = dot(kall_ref[j, :ROWS, :], q_all[...], NT)
        part = jnp.sum(jnp.exp2(scores * (ROOT * LOG2E)), axis=0, keepdims=True)
        return total + jnp.where(key_group(kall_ref, j) <= groups, part, 0.0)

    total = lax.fori_loop(0, SIDE, key_block, jnp.zeros((1, SIDE * ROWS), F32))
    for i in range(SIDE):
        total_ref[i] = total[:, i * ROWS : (i + 1) * ROWS]


def grads_kernel(
    total_ref, q_all, qall_ref, kall_ref,
    inner_ref, dkv_hbm, dq_ref,
    g_all, k_all, v_all, logs, deltas, groups, dq_acc, dkv_buf, sems,
):
    for i in range(SIDE):
        span = slice(i * ROWS, (i + 1) * ROWS)
        g_all[span, :] = qall_ref[i, ROWS : 2 * ROWS, :]
        k_all[span, :] = kall_ref[i, :ROWS, :]
        v_all[span, :] = kall_ref[i, ROWS : 2 * ROWS, :]
        lines = qall_ref[i, 2 * ROWS :, :].astype(F32)
        deltas[:, span] = across(lines, 0) + across(lines, PIECES)
        logs[:, span] = jnp.log2(total_ref[i])
    groups[...] = query_groups(qall_ref)
    dq_acc[...] = jnp.zeros_like(dq_acc)
    half = SIDE * ROWS // 2

    def leave(m):
        pair = pl.ds(2 * m, 2)
        return pltpu.make_async_copy(dkv_buf.at[pair], dkv_hbm.at[pair], sems.at[m])

    def key_pair(m, carry):
        rows = pl.ds(pl.multiple_of(m * half, half), half)
        keys = k_all[rows, :]
        vals = v_all[rows, :]
        shifts = [
            jnp.where(key_group(kall_ref, 2 * m + n) <= groups[...], logs[...], 1e30) for n in range(2)
        ]

        def part(h):
            span = slice(h * half, (h + 1) * half)
            queries = q_all[span, :]
            grad = g_all[span, :]
            scores = dot(keys, queries, NT) * (ROOT * LOG2E)
            upper = scores[:ROWS] - shifts[0][:, span]
            lower = scores[ROWS:] - shifts[1][:, span]
            probs = jnp.exp2(jnp.concatenate([upper, lower], axis=0))
            dprobs = dot(vals, grad, NT)
            dscores = (probs * (dprobs - deltas[:, span])).astype(BF16)
            dq_acc[:, span] += dot(keys, dscores, TN)
            return dot(dscores, queries), dot(probs.astype(BF16), grad)

        first, second = part(0), part(1)
        dk = ((first[0] + second[0]) * ROOT).astype(BF16)
        dv = (first[1] + second[1]).astype(BF16)
        for n in range(2):
            dkv_buf[2 * m + n, :ROWS, :] = dk[n * ROWS : (n + 1) * ROWS]
            dkv_buf[2 * m + n, ROWS:, :] = dv[n * ROWS : (n + 1) * ROWS]
        leave(m).start()
        return carry

    lax.fori_loop(0, SIDE // 2, key_pair, 0)
    for p in range(SIDE * PIECES):
        span = slice(p * WIDTH, (p + 1) * WIDTH)
        product = dq_acc[:, span] * q_all[span, :].astype(F32).T
        inner_ref[:, span] = jnp.sum(product, axis=0, keepdims=True) * ROOT
    for i in range(SIDE):
        dq_ref[i] = (dq_acc[:, i * ROWS : (i + 1) * ROWS].T * ROOT).astype(BF16)
    for m in range(SIDE // 2):
        leave(m).wait()


def sums_kernel(
    place_ref, inner_ref, dkv_ref, dq_ref, k_ref, kscale_ref,
    gk_ref, msg_ref, own_ref, out0_ref, out1_ref, out2_ref, out3_ref,
):
    k_lines = []
    for i in range(PIECES):
        rows = pl.ds(i * WIDTH, WIDTH)
        gk = sum(dkv_ref[j, rows, :].astype(F32) for j in range(SIDE)) * kscale_ref[...]
        gk_ref[rows, :] = gk
        k_lines.append(row_sums(gk * k_ref[rows, :].astype(F32)))
    q_line = jnp.zeros((1, ROWS), F32)
    for i in range(SIDE):
        q_line = jnp.where(place_ref[1] == i, inner_ref[:, i * ROWS : (i + 1) * ROWS], q_line)
    both = jnp.concatenate([q_line, jnp.concatenate(k_lines, axis=1)], axis=0)
    own_ref[...] = both
    coded = both.astype(BF16)
    for h in range(HEADS):
        msg_ref[h] = coded
    for d, target in enumerate((out0_ref, out1_ref, out2_ref, out3_ref)):
        target[...] = dq_ref[place_ref[1] ^ d]


def values_kernel(dkv_ref, gk_ref, rate_ref, dv_ref, scaled_ref):
    for i in range(PIECES):
        rows = pl.ds(i * WIDTH, WIDTH)
        span = slice(i * WIDTH, (i + 1) * WIDTH)
        scaled_ref[rows, :] = column(rate_ref[1:2, span]) * gk_ref[rows, :]
    dv_ref[...] = sum(dkv_ref[j, ROWS:, :].astype(F32) for j in range(SIDE)).astype(BF16)


def final_kernel(
    sums_ref, own_ref, rate_ref, dq0_ref, dq1_ref, dq2_ref, dq3_ref, gk_ref, q_ref, k_ref, qscale_ref,
    dq_hbm, dk_hbm, dq_ref, dk_ref, sems,
):
    inner = own_ref[...] - own_ref[...].astype(BF16).astype(F32)
    for h in range(HEADS):
        inner = inner + sums_ref[h].astype(F32)
    rate = rate_ref[...]
    weight = rate * rate * inner / (HEADS * WIDTH)
    q_weight = weight[0:1, :]
    k_weight = weight[1:2, :] * rate[1:2, :]
    copies = [
        pltpu.make_async_copy(source, target, sems.at[n])
        for n, (source, target) in enumerate(((dk_ref, dk_hbm), (dq_ref, dq_hbm)))
    ]
    for i in range(PIECES):
        rows = pl.ds(i * WIDTH, WIDTH)
        span = slice(i * WIDTH, (i + 1) * WIDTH)
        k = k_ref[rows, :].astype(F32)
        dk_ref[rows, :] = (gk_ref[rows, :] - k * column(k_weight[:, span])).astype(BF16)
    copies[0].start()
    for i in range(PIECES):
        rows = pl.ds(i * WIDTH, WIDTH)
        span = slice(i * WIDTH, (i + 1) * WIDTH)
        gq = sum(part[rows, :].astype(F32) for part in (dq0_ref, dq1_ref, dq2_ref, dq3_ref))
        gq = gq * qscale_ref[...]
        q = q_ref[rows, :].astype(F32)
        dq_ref[rows, :] = (column(rate[0:1, span]) * gq - q * column(q_weight[:, span])).astype(BF16)
    copies[1].start()
    for copy in copies:
        copy.wait()


def local(q_raw, k_raw, values, out, d_out, q_gain, k_gain, order):
    block = struct((ROWS, WIDTH), BF16)
    wide = struct((ROWS, WIDTH), F32)
    pair = struct((2 * ROWS, WIDTH), BF16)
    message = struct((HEADS, 2, ROWS), BF16)
    place = jnp.stack([lax.axis_index("y"), lax.axis_index("x")]).astype(jnp.int32)
    q_gain = q_gain.reshape(1, WIDTH)
    k_gain = k_gain.reshape(1, WIDTH)

    exact = struct((2, ROWS), F32)
    squares, own_squares = call(squares_kernel, (message, exact), limit=60)(q_raw, k_raw)
    squares = lax.all_to_all(squares, HEAD, 0, 0)
    gain = struct((1, WIDTH), F32)
    own_squares, d_out, values, lines, q_gain, k_gain = call(
        ready_kernel,
        (exact, block, block, struct((LINES, WIDTH), BF16), gain, gain),
        spaces="ss",
    )(place, order, own_squares, d_out, out, values, q_gain, k_gain)
    rate, queries, keys = call(
        norms_kernel,
        (
            struct((2, ROWS), F32),
            struct((SIDE, 2 * ROWS + LINES, WIDTH), BF16),
            struct((2 * ROWS + LINES, WIDTH), BF16),
        ),
        scratch=(
            pltpu.VMEM((2 * ROWS + LINES, WIDTH), BF16),
            pltpu.SemaphoreType.DMA((2, SIDE)),
        ),
        out_spaces="vh",
    )(squares, own_squares, q_raw, k_raw, d_out, values, lines, q_gain, k_gain)
    queries = lax.all_to_all(queries, "x", 0, 0)
    keys = lax.all_gather(keys, "y", axis=0, tiled=True).reshape(SIDE, 2 * ROWS + LINES, WIDTH)

    totals, q_all = call(
        totals_kernel, (struct((SIDE, 1, ROWS), F32), struct((SIDE * ROWS, WIDTH), BF16))
    )(queries, keys)
    totals = lax.psum(totals, "x")

    tall = pltpu.VMEM((SIDE * ROWS, WIDTH), BF16)
    row = pltpu.VMEM((1, SIDE * ROWS), F32)
    inner, keys, queries = call(
        grads_kernel,
        (
            struct((1, SIDE * ROWS), F32),
            struct((SIDE, 2 * ROWS, WIDTH), BF16),
            struct((SIDE, ROWS, WIDTH), BF16),
        ),
        scratch=(
            tall, tall, tall, row, row, row,
            pltpu.VMEM((WIDTH, SIDE * ROWS), F32),
            pltpu.VMEM((SIDE, 2 * ROWS, WIDTH), BF16),
            pltpu.SemaphoreType.DMA((SIDE // 2,)),
        ),
        out_spaces="vh",
    )(totals, q_all, queries, keys)
    keys = lax.all_to_all(keys, "y", 0, 0)
    inner = lax.psum(inner, "x")
    gk, inner, own_inner, *queries = call(
        sums_kernel, (wide, message, exact, block, block, block, block), spaces="s"
    )(place, inner, keys, queries, k_raw, k_gain)
    inner = lax.all_to_all(inner, HEAD, 0, 0)
    dv, gk = call(values_kernel, (block, wide))(keys, gk, rate)
    queries[1:] = [swap(part, "x", d) for d, part in enumerate(queries[1:], 1)]
    d_q, d_k = call(
        final_kernel,
        (block, block),
        scratch=(
            pltpu.VMEM((ROWS, WIDTH), BF16),
            pltpu.VMEM((ROWS, WIDTH), BF16),
            pltpu.SemaphoreType.DMA((2,)),
        ),
        out_spaces="hh",
    )(
        inner, own_inner, rate, *queries, gk, q_raw, k_raw, q_gain
    )
    return d_q, d_k, dv


def solution(mesh):
    fine = Mesh(mesh.devices.reshape(SIDE, SIDE, 16, 2), ("y", "x", "z", "c"))
    both = P(SEQ, HEAD)
    return jax.shard_map(
        local,
        mesh=fine,
        in_specs=(both,) * 5 + (P(HEAD), P(HEAD), P()),
        out_specs=(both,) * 3,
        check_vma=False,
    )
```

```python
import math

import jax
import jax.numpy as jnp
from jax import lax
from jax.experimental import pallas as pl
from jax.experimental.pallas import tpu as pltpu
from jax.sharding import Mesh, PartitionSpec as P

EPSILON = 1e-06
SIDE = 4
HEADS = 32
ROWS = 384
WIDTH = 128
PIECES = ROWS // WIDTH
LINES = 16
HEAD = ("z", "c")
SEQ = ("y", "x")
F32 = jnp.float32
BF16 = jnp.bfloat16
ROOT = WIDTH ** (-0.5)
LOG2E = math.log2(math.e)
NT = (((1,), (1,)), ((), ()))
TN = (((0,), (0,)), ((), ()))


def swap(value, axis, mask):
    return lax.ppermute(value, axis, [(i, i ^ mask) for i in range(SIDE)])


def struct(shape, dtype):
    return jax.ShapeDtypeStruct(shape, dtype)


def call(kernel, out_shape, scratch=(), spaces="", out_spaces="", limit=32):
    def run(*args):
        memory = {"s": pltpu.SMEM, "v": pltpu.VMEM, "h": pltpu.HBM}
        leaves, tree = jax.tree.flatten(out_shape)
        out_specs = [
            pl.BlockSpec(memory_space=memory[s]) for s in out_spaces.ljust(len(leaves), "v")
        ]
        specs = [pl.BlockSpec(memory_space=memory[s]) for s in spaces.ljust(len(args), "v")]
        return pl.pallas_call(
            kernel,
            out_shape=out_shape,
            in_specs=specs,
            out_specs=jax.tree.unflatten(tree, out_specs),
            scratch_shapes=scratch,
            compiler_params=pltpu.CompilerParams(vmem_limit_bytes=limit * 2**20),
        )(*args)

    return run


def column(row):
    return jnp.broadcast_to(row, (WIDTH, WIDTH)).T


def row_sums(block):
    return jnp.sum(block.T, axis=0, keepdims=True)


def dot(a, b, dims=(((1,), (0,)), ((), ()))):
    return lax.dot_general(a, b, dims, preferred_element_type=F32)


def encode(value):
    square = value * value
    return (square * square).astype(BF16)


def decode(coded):
    return lax.rsqrt(lax.rsqrt(jnp.maximum(coded.astype(F32), 1e-36)))


def squares_kernel(q_ref, k_ref, msg_ref, own_ref):
    ones = jnp.ones((16, WIDTH), BF16)
    sums = []
    for ref in (q_ref, k_ref):
        value = ref[...].astype(F32)
        square = value * value
        high = square.astype(BF16)
        low = (square - high.astype(F32)).astype(BF16)
        sums.append((dot(ones, high, NT) + dot(ones, low, NT))[:1, :])
    both = jnp.concatenate(sums, axis=0)
    own_ref[...] = both
    coded = encode(both)
    for h in range(HEADS):
        msg_ref[h] = coded


def ready_kernel(
    place_ref, order_ref, own_ref, g_ref, o_ref, v_ref, qgain_ref, kgain_ref,
    own_out, g_out, v_out, lines_ref, qscale_ref, kscale_ref,
):
    group = order_ref[place_ref[0] * SIDE + place_ref[1]].astype(F32)
    line = lax.broadcasted_iota(jnp.int32, (LINES, WIDTH), 0)
    lines = jnp.full((LINES, WIDTH), group, F32)
    for i in range(PIECES):
        rows = pl.ds(i * WIDTH, WIDTH)
        delta = row_sums(o_ref[rows, :].astype(F32) * g_ref[rows, :].astype(F32))
        high = delta.astype(BF16).astype(F32)
        lines = jnp.where(line == i, high, lines)
        lines = jnp.where(line == PIECES + i, delta - high, lines)
    lines_ref[...] = lines.astype(BF16)
    own_out[...] = own_ref[...]
    g_out[...] = g_ref[...]
    v_out[...] = v_ref[...]
    qscale_ref[...] = qgain_ref[...].astype(F32)
    kscale_ref[...] = kgain_ref[...].astype(F32)


def norms_kernel(
    sums_ref, own_ref, q_ref, k_ref, g_ref, v_ref, lines_ref, qscale_ref, kscale_ref,
    rate_ref, qmsg_hbm, kmsg_ref, q_buf, sems,
):
    early = pl.ds(ROWS, ROWS + LINES)
    late = pl.ds(0, ROWS)
    copies = [
        [
            pltpu.make_async_copy(q_buf.at[rows, :], qmsg_hbm.at[x, rows, :], sems.at[n, x])
            for x in range(SIDE)
        ]
        for n, rows in enumerate((early, late))
    ]
    q_buf[ROWS : 2 * ROWS, :] = g_ref[...]
    q_buf[2 * ROWS :, :] = lines_ref[...]
    for copy in copies[0]:
        copy.start()
    total = own_ref[...] - decode(encode(own_ref[...]))
    for h in range(HEADS):
        total = total + decode(sums_ref[h])
    total = jnp.maximum(total, own_ref[...])
    rate = lax.rsqrt(total / (HEADS * WIDTH) + EPSILON)
    rate_ref[...] = rate
    for i in range(PIECES):
        rows = pl.ds(i * WIDTH, WIDTH)
        span = slice(i * WIDTH, (i + 1) * WIDTH)
        q = q_ref[rows, :].astype(F32) * column(rate[0:1, span]) * qscale_ref[...]
        q_buf[rows, :] = q.astype(BF16)
    for copy in copies[1]:
        copy.start()
    for i in range(PIECES):
        rows = pl.ds(i * WIDTH, WIDTH)
        span = slice(i * WIDTH, (i + 1) * WIDTH)
        k = k_ref[rows, :].astype(F32) * column(rate[1:2, span]) * kscale_ref[...]
        kmsg_ref[rows, :] = k.astype(BF16)
    kmsg_ref[ROWS : 2 * ROWS, :] = v_ref[...]
    kmsg_ref[2 * ROWS :, :] = lines_ref[...]
    for copy in copies[0] + copies[1]:
        copy.wait()


def across(lines, first):
    return jnp.concatenate([lines[first + p : first + p + 1, :] for p in range(PIECES)], axis=1)


def query_groups(qall_ref):
    rows = [qall_ref[i, 2 * ROWS :, :].astype(F32)[2 * PIECES : 2 * PIECES + 1, :] for i in range(SIDE)]
    return jnp.concatenate([row for row in rows for _ in range(PIECES)], axis=1)


def key_group(kall_ref, j):
    row = kall_ref[j, 2 * ROWS :, :].astype(F32)[2 * PIECES : 2 * PIECES + 1, :]
    return jnp.concatenate([row] * (SIDE * PIECES), axis=1)


def totals_kernel(qall_ref, kall_ref, total_ref, q_all):
    for i in range(SIDE):
        q_all[i * ROWS : (i + 1) * ROWS, :] = qall_ref[i, :ROWS, :]
    groups = query_groups(qall_ref)

    def key_block(j, total):
        scores = dot(kall_ref[j, :ROWS, :], q_all[...], NT)
        part = jnp.sum(jnp.exp2(scores * (ROOT * LOG2E)), axis=0, keepdims=True)
        return total + jnp.where(key_group(kall_ref, j) <= groups, part, 0.0)

    total = lax.fori_loop(0, SIDE, key_block, jnp.zeros((1, SIDE * ROWS), F32))
    for i in range(SIDE):
        total_ref[i] = total[:, i * ROWS : (i + 1) * ROWS]


def grads_kernel(
    total_ref, qall_ref, kall_ref,
    inner_ref, dkv_hbm, dq_ref,
    q_all, g_all, k_all, v_all, logs, deltas, groups, dq_acc, dkv_buf, sems,
):
    for i in range(SIDE):
        span = slice(i * ROWS, (i + 1) * ROWS)
        q_all[span, :] = qall_ref[i, :ROWS, :]
        g_all[span, :] = qall_ref[i, ROWS : 2 * ROWS, :]
        k_all[span, :] = kall_ref[i, :ROWS, :]
        v_all[span, :] = kall_ref[i, ROWS : 2 * ROWS, :]
        lines = qall_ref[i, 2 * ROWS :, :].astype(F32)
        deltas[:, span] = across(lines, 0) + across(lines, PIECES)
        logs[:, span] = jnp.log2(total_ref[i])
    groups[...] = query_groups(qall_ref)
    dq_acc[...] = jnp.zeros_like(dq_acc)
    half = SIDE * ROWS // 2

    def leave(m):
        pair = pl.ds(2 * m, 2)
        return pltpu.make_async_copy(dkv_buf.at[pair], dkv_hbm.at[pair], sems.at[m])

    def key_pair(m, carry):
        rows = pl.ds(pl.multiple_of(m * half, half), half)
        keys = k_all[rows, :]
        vals = v_all[rows, :]
        shifts = [
            jnp.where(key_group(kall_ref, 2 * m + n) <= groups[...], logs[...], 1e30) for n in range(2)
        ]

        def part(h):
            span = slice(h * half, (h + 1) * half)
            queries = q_all[span, :]
            grad = g_all[span, :]
            scores = dot(keys, queries, NT) * (ROOT * LOG2E)
            upper = scores[:ROWS] - shifts[0][:, span]
            lower = scores[ROWS:] - shifts[1][:, span]
            probs = jnp.exp2(jnp.concatenate([upper, lower], axis=0))
            dprobs = dot(vals, grad, NT)
            dscores = (probs * (dprobs - deltas[:, span])).astype(BF16)
            dq_acc[:, span] += dot(keys, dscores, TN)
            return dot(dscores, queries), dot(probs.astype(BF16), grad)

        first, second = part(0), part(1)
        dk = ((first[0] + second[0]) * ROOT).astype(BF16)
        dv = (first[1] + second[1]).astype(BF16)
        for n in range(2):
            dkv_buf[2 * m + n, :ROWS, :] = dk[n * ROWS : (n + 1) * ROWS]
            dkv_buf[2 * m + n, ROWS:, :] = dv[n * ROWS : (n + 1) * ROWS]
        leave(m).start()
        return carry

    lax.fori_loop(0, SIDE // 2, key_pair, 0)
    for p in range(SIDE * PIECES):
        span = slice(p * WIDTH, (p + 1) * WIDTH)
        product = dq_acc[:, span] * q_all[span, :].astype(F32).T
        inner_ref[:, span] = jnp.sum(product, axis=0, keepdims=True) * ROOT
    for i in range(SIDE):
        dq_ref[i] = (dq_acc[:, i * ROWS : (i + 1) * ROWS].T * ROOT).astype(BF16)
    for m in range(SIDE // 2):
        leave(m).wait()


def sums_kernel(
    place_ref, inner_ref, dkv_ref, dq_ref, k_ref, kscale_ref,
    gk_ref, msg_ref, own_ref, out0_ref, out1_ref, out2_ref, out3_ref,
):
    k_lines = []
    for i in range(PIECES):
        rows = pl.ds(i * WIDTH, WIDTH)
        gk = sum(dkv_ref[j, rows, :].astype(F32) for j in range(SIDE)) * kscale_ref[...]
        gk_ref[rows, :] = gk
        k_lines.append(row_sums(gk * k_ref[rows, :].astype(F32)))
    q_line = jnp.zeros((1, ROWS), F32)
    for i in range(SIDE):
        q_line = jnp.where(place_ref[1] == i, inner_ref[:, i * ROWS : (i + 1) * ROWS], q_line)
    both = jnp.concatenate([q_line, jnp.concatenate(k_lines, axis=1)], axis=0)
    own_ref[...] = both
    coded = both.astype(BF16)
    for h in range(HEADS):
        msg_ref[h] = coded
    for d, target in enumerate((out0_ref, out1_ref, out2_ref, out3_ref)):
        target[...] = dq_ref[place_ref[1] ^ d]


def values_kernel(dkv_ref, dv_ref):
    dv_ref[...] = sum(dkv_ref[j, ROWS:, :].astype(F32) for j in range(SIDE)).astype(BF16)


def final_kernel(
    sums_ref, own_ref, rate_ref, dq0_ref, dq1_ref, dq2_ref, dq3_ref, gk_ref, q_ref, k_ref, qscale_ref,
    dq_ref, dk_ref,
):
    inner = own_ref[...] - own_ref[...].astype(BF16).astype(F32)
    for h in range(HEADS):
        inner = inner + sums_ref[h].astype(F32)
    rate = rate_ref[...]
    weight = rate * rate * inner / (HEADS * WIDTH)
    q_weight = weight[0:1, :]
    k_weight = weight[1:2, :] * rate[1:2, :]
    for i in range(PIECES):
        rows = pl.ds(i * WIDTH, WIDTH)
        span = slice(i * WIDTH, (i + 1) * WIDTH)
        gq = sum(part[rows, :].astype(F32) for part in (dq0_ref, dq1_ref, dq2_ref, dq3_ref))
        gq = gq * qscale_ref[...]
        gk = gk_ref[rows, :]
        q = q_ref[rows, :].astype(F32)
        k = k_ref[rows, :].astype(F32)
        dq_ref[rows, :] = (column(rate[0:1, span]) * gq - q * column(q_weight[:, span])).astype(BF16)
        dk_ref[rows, :] = (column(rate[1:2, span]) * gk - k * column(k_weight[:, span])).astype(BF16)


def local(q_raw, k_raw, values, out, d_out, q_gain, k_gain, order):
    block = struct((ROWS, WIDTH), BF16)
    wide = struct((ROWS, WIDTH), F32)
    pair = struct((2 * ROWS, WIDTH), BF16)
    message = struct((HEADS, 2, ROWS), BF16)
    place = jnp.stack([lax.axis_index("y"), lax.axis_index("x")]).astype(jnp.int32)
    q_gain = q_gain.reshape(1, WIDTH)
    k_gain = k_gain.reshape(1, WIDTH)

    exact = struct((2, ROWS), F32)
    squares, own_squares = call(squares_kernel, (message, exact), limit=60)(q_raw, k_raw)
    squares = lax.all_to_all(squares, HEAD, 0, 0)
    gain = struct((1, WIDTH), F32)
    own_squares, d_out, values, lines, q_gain, k_gain = call(
        ready_kernel,
        (exact, block, block, struct((LINES, WIDTH), BF16), gain, gain),
        spaces="ss",
    )(place, order, own_squares, d_out, out, values, q_gain, k_gain)
    rate, queries, keys = call(
        norms_kernel,
        (
            struct((2, ROWS), F32),
            struct((SIDE, 2 * ROWS + LINES, WIDTH), BF16),
            struct((2 * ROWS + LINES, WIDTH), BF16),
        ),
        scratch=(
            pltpu.VMEM((2 * ROWS + LINES, WIDTH), BF16),
            pltpu.SemaphoreType.DMA((2, SIDE)),
        ),
        out_spaces="vh",
    )(squares, own_squares, q_raw, k_raw, d_out, values, lines, q_gain, k_gain)
    queries = lax.all_to_all(queries, "x", 0, 0)
    keys = lax.all_gather(keys, "y", axis=0, tiled=True).reshape(SIDE, 2 * ROWS + LINES, WIDTH)

    totals = call(
        totals_kernel,
        struct((SIDE, 1, ROWS), F32),
        scratch=(pltpu.VMEM((SIDE * ROWS, WIDTH), BF16),),
    )(queries, keys)
    totals = lax.psum(totals, "x")

    tall = pltpu.VMEM((SIDE * ROWS, WIDTH), BF16)
    row = pltpu.VMEM((1, SIDE * ROWS), F32)
    inner, keys, queries = call(
        grads_kernel,
        (
            struct((1, SIDE * ROWS), F32),
            struct((SIDE, 2 * ROWS, WIDTH), BF16),
            struct((SIDE, ROWS, WIDTH), BF16),
        ),
        scratch=(
            tall, tall, tall, tall, row, row, row,
            pltpu.VMEM((WIDTH, SIDE * ROWS), F32),
            pltpu.VMEM((SIDE, 2 * ROWS, WIDTH), BF16),
            pltpu.SemaphoreType.DMA((SIDE // 2,)),
        ),
        out_spaces="vh",
    )(totals, queries, keys)
    keys = lax.all_to_all(keys, "y", 0, 0)
    inner = lax.psum(inner, "x")
    dv = call(values_kernel, block)(keys)
    gk, inner, own_inner, *queries = call(
        sums_kernel, (wide, message, exact, block, block, block, block), spaces="s"
    )(place, inner, keys, queries, k_raw, k_gain)
    inner = lax.all_to_all(inner, HEAD, 0, 0)
    queries[1:] = [swap(part, "x", d) for d, part in enumerate(queries[1:], 1)]
    d_q, d_k = call(final_kernel, (block, block))(
        inner, own_inner, rate, *queries, gk, q_raw, k_raw, q_gain
    )
    return d_q, d_k, dv


def solution(mesh):
    fine = Mesh(mesh.devices.reshape(SIDE, SIDE, 16, 2), ("y", "x", "z", "c"))
    both = P(SEQ, HEAD)
    return jax.shard_map(
        local,
        mesh=fine,
        in_specs=(both,) * 5 + (P(HEAD), P(HEAD), P()),
        out_specs=(both,) * 3,
        check_vma=False,
    )
```
